32 devices in a mesh: dom: 16 (over z, y, x), grp: 2 (over core).
Axes of the slice: x: 2, y: 2, z: 4, core: 2. Of those that a mesh axis runs over, the one named last changes fastest.
Arguments:
- source: float32 [512, 64, 128], P('dom', 'grp'), may hold values from -48 to 48
- conductivity: float32 [512, 64, 128], P('dom', 'grp'), may hold values from 0.3 to 3
- absorption: float32 [512, 64, 128], P('dom', 'grp'), may hold values from 0.1 to 2
- brick_mask: int32 [64, 8, 16], P('dom', 'grp'), may hold values 0 or 1
Outputs:
- fine_iterate: float32 [512, 64, 128], P('dom', 'grp')
- fine_residual: float32 [512, 64, 128], P('dom', 'grp')
- mid_iterate: float32 [256, 32, 64], P('dom', 'grp')
- coarse_iterate: float32 [128, 16, 32], P('dom', 'grp')
The draws below stay inside these ranges and needn't reach their ends.
All inputs are finite; a program needn't handle non-finite values. No bound on the sum of `brick_mask` on one device may be relied on, other than what follows from the above.
Results may differ from the reference program's by a relative error of at most 0.00002.
Values sent between devices are 32-bit elements; how exact they have to be, the bound alone decides.
No kernel may reach another device: no remote copies, remote signals or barrier semaphores. Data moves between devices by JAX's collectives and lax.ppermute only.
A program may use at most 192 MiB of HBM per device.

```python
import math
import jax
import jax.numpy as jnp

DEGREE = 4
COARSE_DEGREE = 6
NX = 512
NY = 64
NZ = 128
NBX = 64
NBY = 8
NBZ = 16


def set_ends(drawn, own_key, smallest, high):
    index_at = [jax.random.randint(jax.random.fold_in(own_key, axis), (), 0, length) for axis, length in enumerate(drawn.shape)]
    widest = drawn.shape.index(max(drawn.shape))
    beside = index_at[:widest] + [(index_at[widest] + 1) % drawn.shape[widest]] + index_at[widest + 1:]
    return drawn.at[tuple(index_at)].set(smallest).at[tuple(beside)].set(high)


def steps_of(key, shape, cuts, least, top_value):
    level = 1.0
    for axis_at, shards_of in cuts:
        heights = jax.random.uniform(jax.random.fold_in(jax.random.fold_in(key, 6), axis_at), (shards_of,), jnp.float32, least / len(cuts), top_value / len(cuts))
        level = level * jnp.repeat(jnp.exp(heights), shape[axis_at] // shards_of).reshape((-1,) + (1,) * (len(shape) - 1 - axis_at))
    return level


def centred(key, extent, scale, limit, pieces=(), kind=jnp.bfloat16):
    factor_of = steps_of(key, extent, pieces, -0.22, 0.18) if pieces else 1.0
    values = jax.random.normal(key, extent, jnp.float32) * scale * factor_of
    return jnp.minimum(jnp.maximum(values, -limit), limit).astype(kind)


def setup_inputs(seed: int = 0) -> dict:
    splits = jax.random.split(jax.random.key(seed), 5)
    source = centred(splits[0], (NX, NY, NZ), 8.0, 48.0, ((0, 16), (1, 2)), jnp.float32)
    conductivity = jnp.clip(jnp.exp(math.log(3.0) - 2.3025851 * jax.random.uniform(splits[1], (NX, NY, NZ), jnp.float32) ** steps_of(splits[1], (NX, NY, NZ), ((0, 16), (1, 2)), -0.2, 0.2)), 0.3, 3.0)
    absorption = jnp.clip(jnp.exp(math.log(2.0) - 2.9957323 * jax.random.uniform(splits[2], (NX, NY, NZ), jnp.float32) ** steps_of(splits[2], (NX, NY, NZ), ((0, 16), (1, 2)), -0.2, 0.2)), 0.1, 2.0)
    brick_mask = set_ends((jax.random.randint(splits[3], (NBX, NBY, NBZ), 0, 4) < 3).astype(jnp.int32), jax.random.fold_in(splits[3], 1), 0, 1)
    return {"source": source, "conductivity": conductivity, "absorption": absorption, "brick_mask": brick_mask}


step_scale = 4.0
smooth_low = 0.3
smooth_high = 2.0
coarse_low = 0.05


def refine_mask(brick_flags):
    values = brick_flags.astype(jnp.float32)
    values = jnp.repeat(values, 8, axis=0)
    values = jnp.repeat(values, 8, axis=1)
    return jnp.repeat(values, 8, axis=2)


def six_views(padded):
    return [padded[2:, 1:-1, 1:-1], padded[:-2, 1:-1, 1:-1],
            padded[1:-1, 2:, 1:-1], padded[1:-1, :-2, 1:-1],
            padded[1:-1, 1:-1, 2:], padded[1:-1, 1:-1, :-2]]


def coefficients(kappa_pad, filled_pad, absorb_cells, factor):
    kappa_mid = kappa_pad[1:-1, 1:-1, 1:-1]
    weights = []
    summed = jnp.zeros_like(kappa_mid)
    counted = jnp.zeros_like(kappa_mid)
    for neighbour_kappa, neighbour_filled in zip(six_views(kappa_pad), six_views(filled_pad)):
        weight = factor * 0.5 * (kappa_mid + neighbour_kappa) * neighbour_filled
        weights.append(weight)
        summed = summed + weight
        counted = counted + neighbour_filled
    diagonal = 1.0 + summed + factor * absorb_cells * (6.0 - counted)
    return weights, diagonal


def apply_padded(field_pad, weights, diagonal, filled):
    center = field_pad[1:-1, 1:-1, 1:-1]
    neighbours = six_views(field_pad)
    coupled = weights[0] * neighbours[0]
    for index in range(1, 6):
        coupled = coupled + weights[index] * neighbours[index]
    return filled * (diagonal * center - coupled) + (1.0 - filled) * center


def chebyshev(source_term, diagonal, degree, lowest, highest, operate, keep_residual):
    middle = (highest + lowest) / 2.0
    spread = (highest - lowest) / 2.0
    relative = middle / spread
    factor_prev = 1.0 / relative
    inverse = 1.0 / diagonal
    update = (inverse * source_term) / middle
    iterate = update
    residual = source_term
    for sweep_index in range(degree):
        if sweep_index > 0:
            factor_next = 1.0 / (2.0 * relative - factor_prev)
            update = (factor_next * factor_prev) * update + (2.0 * factor_next / spread) * (inverse * residual)
            iterate = iterate + update
            factor_prev = factor_next
        if sweep_index < degree - 1 or keep_residual:
            residual = residual - operate(update)
    return iterate, residual


def coarsen(fields):
    shape_in = fields.shape
    blocks = fields.reshape(shape_in[0] // 2, 2, shape_in[1] // 2, 2, shape_in[2] // 2, 2)
    return jnp.mean(blocks, axis=(1, 3, 5))


def level_solve(source_term, kappa, absorb, filled, factor, degree, lowest, keep_residual):
    weights, diagonal = coefficients(jnp.pad(kappa, 1), jnp.pad(filled, 1), absorb, factor)

    def operate(vector):
        return apply_padded(jnp.pad(vector, 1), weights, diagonal, filled)

    return chebyshev(source_term, diagonal, degree, lowest, smooth_high, operate, keep_residual)


def reference(source, conductivity, absorption, brick_mask):
    filled = refine_mask(brick_mask)
    fine_iterate, fine_residual = level_solve(source * filled, conductivity, absorption, filled,
                                              step_scale, DEGREE, smooth_low, True)
    mid_kappa = coarsen(conductivity)
    mid_absorb = coarsen(absorption)
    mid_filled = coarsen(filled)
    mid_iterate, mid_residual = level_solve(coarsen(fine_residual), mid_kappa, mid_absorb, mid_filled,
                                            step_scale / 4.0, DEGREE, smooth_low, True)
    coarse_iterate = level_solve(coarsen(mid_residual), coarsen(mid_kappa), coarsen(mid_absorb),
                                 coarsen(mid_filled), step_scale / 16.0, COARSE_DEGREE, coarse_low, False)[0]
    return (fine_iterate, fine_residual, mid_iterate, coarse_iterate)
```

```python
import functools

import jax
import jax.numpy as jnp
from jax import lax
from jax.experimental import pallas as pl
from jax.experimental.pallas import tpu as pltpu
from jax.sharding import PartitionSpec as P

DEGREE = 4
COARSE_DEGREE = 6

STEP_SCALE = 4.0
SMOOTH_LOW = 0.3
SMOOTH_HIGH = 2.0
COARSE_LOW = 0.05

BRICK = 8
TILE = 8
VMEM_BYTES = 48 * 1024 * 1024


def chebyshev_constants(degree, lowest, highest):
    middle = (highest + lowest) / 2.0
    spread = (highest - lowest) / 2.0
    relative = middle / spread
    previous = 1.0 / relative
    steps = []
    for _ in range(degree - 1):
        following = 1.0 / (2.0 * relative - previous)
        steps.append((following * previous, 2.0 * following / spread))
        previous = following
    return 1.0 / middle, steps


def lane_index(shape):
    return lax.broadcasted_iota(jnp.int32, shape, len(shape) - 1)


def ahead(value, axis, step=1):
    return pltpu.roll(value, value.shape[axis] - step, axis)


def behind(value, axis, step=1):
    return pltpu.roll(value, step, axis)


def positive(value):
    return jnp.where(value > 0.0, 1.0, 0.0)


def rows_loop(start, stop, body, unroll=2):
    lax.fori_loop(start, stop, lambda i, c: (body(i), c)[1], 0, unroll=unroll)


def level_setup(lo, hi, zstep, factor, g_ref, a_ref, wx_ref, wy_ref, wz_ref, inv_ref, d_ref):
    half = 0.5 * factor

    def weight_x(i):
        here, there = g_ref[i], g_ref[i + 1]
        wx_ref[i] = jnp.where((here > 0.0) & (there > 0.0), half * (here + there), 0.0)

    weight_x(lo - 1)

    def row(i):
        weight_x(i)
        here = g_ref[i]
        lanes = lane_index(here.shape)
        inside = here > 0.0
        there_y = ahead(here, 0)
        there_z = ahead(here, 1, zstep)
        wy = jnp.where(inside & (there_y > 0.0), half * (here + there_y), 0.0)
        wz = jnp.where(inside & (there_z > 0.0) & (lanes < here.shape[1] - zstep), half * (here + there_z), 0.0)
        wy_ref[i] = wy
        wz_ref[i] = wz
        faces = [wx_ref[i], wx_ref[i - 1], wy, behind(wy, 0), wz, behind(wz, 1, zstep)]
        summed = faces[0]
        counted = positive(faces[0])
        for face in faces[1:]:
            summed = summed + face
            counted = counted + positive(face)
        diagonal = 1.0 + summed + factor * a_ref[i] * (6.0 - counted)
        d_ref[i] = diagonal
        inv_ref[i] = jnp.where(inside, 1.0 / diagonal, 0.0)

    rows_loop(lo, hi, row)


def level_sweeps(base, size, reach, degree, lowest, keep, zstep, b_ref, inv_ref, wx_ref, wy_ref, wz_ref, e_ref, u_refs):
    first, steps = chebyshev_constants(degree, lowest, SMOOTH_HIGH)
    passes = degree if keep else degree - 1

    def start(i):
        e = inv_ref[i] * b_ref[i]
        e_ref[i] = e
        u_refs[0][i] = e * first

    width = reach + passes
    rows_loop(base - width, base + size + width, start)
    for k in range(passes):
        old = u_refs[k]

        def row(i, k=k, old=old):
            u = old[i]
            wy = wy_ref[i]
            wz = wz_ref[i]
            coupled = wx_ref[i] * old[i + 1] + wx_ref[i - 1] * old[i - 1]
            coupled = coupled + (wy * ahead(u, 0) + behind(wy * u, 0))
            coupled = coupled + (wz * ahead(u, 1, zstep) + behind(wz * u, 1, zstep))
            e = e_ref[i] - u + inv_ref[i] * coupled
            e_ref[i] = e
            if k + 1 < degree:
                u_refs[k + 1][i] = steps[k][0] * u + steps[k][1] * e

        width = reach + passes - 1 - k
        rows_loop(base - width, base + size + width, row)


def coarsen_rows(one, two, pair_ref, zstep):
    pair_ref[...] = one + two
    half = pair_ref.shape[0] // 2
    summed = pair_ref[pl.ds(0, half, 2), :] + pair_ref[pl.ds(1, half, 2), :]
    return (summed + ahead(summed, 1, zstep)) * 0.125


def pack_two(one, two):
    return jnp.where(lane_index(one.shape) % 2 == 0, one, behind(two, 1))


def unpack_two(packed):
    even = lane_index(packed.shape) % 2 == 0
    return jnp.where(even, packed, 0.0), jnp.where(even, ahead(packed, 1), 0.0)


def pack_kernel(slots, src_ref, kap_ref, ab_ref, brick_ref, g_ref, a_out, b_out, q_ref, *rest):
    y_outs, pair_ref = rest[:slots], rest[slots]
    nx, ny, nz = src_ref.shape
    lower, upper = DEGREE, DEGREE + 1
    nbz = brick_ref.shape[2]
    spread = jnp.where(
        lax.broadcasted_iota(jnp.int32, (nbz, nz), 1) // BRICK == lax.broadcasted_iota(jnp.int32, (nbz, nz), 0), 1.0, 0.0
    )
    for bx in range(nx // BRICK):
        lines = jnp.dot(brick_ref[bx].astype(jnp.float32), spread, preferred_element_type=jnp.float32)
        mask = jnp.concatenate(
            [jnp.broadcast_to(lines[by : by + 1], (BRICK, nz)) for by in range(ny // BRICK)], axis=0
        )
        for x in range(bx * BRICK, (bx + 1) * BRICK):
            g_ref[x] = kap_ref[x] * mask

    def packed_pair(ref, j):
        cells = [coarsen_rows(ref[4 * j + 2 * t], ref[4 * j + 2 * t + 1], pair_ref.at[t], 1) for t in range(2)]
        return pack_two(*cells)

    def quad(j):
        q_ref[0, j] = packed_pair(g_ref, j)
        q_ref[1, j] = packed_pair(ab_ref, j)

    rows_loop(0, nx // 4, quad, unroll=True)

    even = lax.axis_index("dom") % 2 == 0
    for out, up in ((a_out, even), (b_out, jnp.logical_not(even))):
        four = jnp.where(up, nx - lower, 0)
        five = jnp.where(up, nx - upper, 0)
        for j in range(lower):
            out[j] = src_ref[four + j]
            out[lower + j] = ab_ref[four + j]
        for j in range(upper):
            out[2 * lower + j] = g_ref[five + j]

    core = lax.axis_index("grp")
    for slot, out in enumerate(y_outs):
        up = core == 0 if slots == 1 else slot == 1
        at = pl.multiple_of(jnp.where(up, ny - TILE, 0), TILE)
        for x in range(nx):
            out[0, x] = src_ref[x, pl.ds(at, TILE), :]
            out[1, x] = ab_ref[x, pl.ds(at, TILE), :]
            out[2, x] = g_ref[x, pl.ds(at, TILE), :]


def slot_is_upper(slots, slot):
    return lax.axis_index("grp") == 0 if slots == 1 else slot == 0


def keep_near(value, is_upper, reach):
    rows = lax.broadcasted_iota(jnp.int32, value.shape, 0)
    size = value.shape[0]
    low = jnp.where(is_upper, 0, size - reach)
    high = jnp.where(is_upper, reach, size)
    return jnp.where((rows >= low) & (rows < high), value, 0.0)


def fine_kernel(slots, src_ref, ab_ref, g_in, ra_ref, rb_ref, *rest):
    y_refs, ya_refs, yb_refs = rest[:slots], rest[slots : 2 * slots], rest[2 * slots : 3 * slots]
    it_out, res_out, s_out = rest[3 * slots : 3 * slots + 3]
    b_ref, a_ref, g_ref, wx, wy, wz, inv, d_ref, e_ref, u0, u1, u2, u3, pair_ref = rest[3 * slots + 3 :]
    nx, ny, nz = src_ref.shape
    lower, upper = DEGREE, DEGREE + 1
    base = upper

    def own(i):
        b_ref[base + i, :ny] = src_ref[i]
        a_ref[base + i, :ny] = ab_ref[i]
        g_ref[base + i, :ny] = g_in[i]
        for slot, y_ref in enumerate(y_refs):
            at = slice(ny + slot * TILE, ny + (slot + 1) * TILE)
            b_ref[base + i, at] = y_ref[0, i]
            a_ref[base + i, at] = y_ref[1, i]
            g_ref[base + i, at] = keep_near(y_ref[2, i], slot_is_upper(slots, slot), upper)

    rows_loop(0, nx, own)

    even = lax.axis_index("dom") % 2 == 0
    for r_ref, y_list, is_above in ((ra_ref, ya_refs, even), (rb_ref, yb_refs, jnp.logical_not(even))):
        four = jnp.where(is_above, base + nx, base - lower)
        five = jnp.where(is_above, base + nx, base - upper)
        for j in range(lower):
            b_ref[four + j, :ny] = r_ref[j]
            a_ref[four + j, :ny] = r_ref[lower + j]
        for j in range(upper):
            g_ref[five + j, :ny] = r_ref[2 * lower + j]
        for slot, y_ref in enumerate(y_list):
            at = slice(ny + slot * TILE, ny + (slot + 1) * TILE)
            is_upper = slot_is_upper(slots, slot)
            part = pl.ds(pl.multiple_of(jnp.where(is_upper, 0, ny - TILE), TILE), TILE)
            for j in range(lower):
                b_ref[four + j, at] = y_ref[j, part, :]
                a_ref[four + j, at] = y_ref[lower + j, part, :]
            for j in range(upper):
                g_ref[five + j, at] = keep_near(y_ref[2 * lower + j, part, :], is_upper, upper)

    level_setup(base - lower, base + nx + lower, 1, STEP_SCALE, g_ref, a_ref, wx, wy, wz, inv, d_ref)
    u_refs = (u0, u1, u2, u3)
    level_sweeps(base, nx, 0, DEGREE, SMOOTH_LOW, True, 1, b_ref, inv, wx, wy, wz, e_ref, u_refs)

    def finish(i):
        total = u_refs[0][base + i, :ny]
        for u_ref in u_refs[1:]:
            total = total + u_ref[base + i, :ny]
        it_out[i] = total
        res_out[i] = d_ref[base + i, :ny] * e_ref[base + i, :ny]

    rows_loop(0, nx, finish)

    def quad(j):
        cells = [
            coarsen_rows(res_out[4 * j + 2 * t], res_out[4 * j + 2 * t + 1], pair_ref.at[t], 1) for t in range(2)
        ]
        s_out[j] = pack_two(*cells)

    rows_loop(0, nx // 4, quad, unroll=True)


def compact(value, step):
    nz = value.shape[-1]
    shape = (nz, nz // step)
    pick = jnp.where(
        lax.broadcasted_iota(jnp.int32, shape, 0) == step * lax.broadcasted_iota(jnp.int32, shape, 1), 1.0, 0.0
    )
    return jnp.dot(value, pick, preferred_element_type=jnp.float32, precision=lax.Precision.HIGHEST)


def coarse_kernel(slots, *refs):
    parts = 3 * (1 + slots)
    q_refs, s_refs = refs[:parts], refs[parts : 2 * parts]
    mid_out, coarse_out = refs[2 * parts : 2 * parts + 2]
    scratch = refs[2 * parts + 2 :]
    b_ref, a_ref, g_ref, wx, wy, wz, inv, d_ref, e_ref, u0, u1, u2, u3 = scratch[:13]
    cb, ca, cg, cwx, cwy, cwz, cinv, cd, ce, v0, v1, v2, v3, v4, v5 = scratch[13:28]
    pair_ref = scratch[28]
    packed, ny, nz = s_refs[0].shape
    nx = 2 * packed
    base = nx
    even = lax.axis_index("dom") % 2 == 0

    for part in range(3):
        start = base if part == 0 else jnp.where(even if part == 1 else jnp.logical_not(even), 2 * nx, 0)
        for slot in range(1 + slots):
            q_ref, s_ref = q_refs[part * (1 + slots) + slot], s_refs[part * (1 + slots) + slot]
            at = slice(slot * ny, (slot + 1) * ny)

            def place(j, q_ref=q_ref, s_ref=s_ref, at=at, start=start, slot=slot):
                g_rows, a_rows, b_rows = unpack_two(q_ref[0, j]), unpack_two(q_ref[1, j]), unpack_two(s_ref[j])
                for t in range(2):
                    g_row = g_rows[t]
                    if slot:
                        g_row = keep_near(g_row, slot_is_upper(slots, slot - 1), ny - 1)
                    g_ref[start + 2 * j + t, at] = g_row
                    a_ref[start + 2 * j + t, at] = a_rows[t]
                    b_ref[start + 2 * j + t, at] = b_rows[t]

            rows_loop(0, packed, place)

    reach = 2 * (COARSE_DEGREE - 1)
    width = reach + DEGREE
    u_refs = (u0, u1, u2, u3)
    level_setup(base - width, base + nx + width, 2, STEP_SCALE / 4.0, g_ref, a_ref, wx, wy, wz, inv, d_ref)
    level_sweeps(base, nx, reach, DEGREE, SMOOTH_LOW, True, 2, b_ref, inv, wx, wy, wz, e_ref, u_refs)

    total = u0[base : base + nx, :ny]
    for u_ref in u_refs[1:]:
        total = total + u_ref[base : base + nx, :ny]
    mid_out[...] = compact(total.reshape(nx * ny, nz), 2).reshape(nx, ny, nz // 2)

    half, cny = nx // 2, ny // 2
    cbase = COARSE_DEGREE
    offset = base - 2 * cbase

    def coefficients(i):
        row = offset + 2 * i
        g0, g1 = g_ref[row], g_ref[row + 1]
        whole = coarsen_rows(positive(g0), positive(g1), pair_ref, 2) > 0.75
        first = lane_index(whole.shape) % 4 == 0
        cg[i] = jnp.where(whole & first, coarsen_rows(g0, g1, pair_ref, 2), 0.0)
        ca[i] = coarsen_rows(a_ref[row], a_ref[row + 1], pair_ref, 2)

    rows_loop(0, half + 2 * cbase, coefficients)

    def source(i):
        row = offset + 2 * i
        cb[i] = coarsen_rows(d_ref[row] * e_ref[row], d_ref[row + 1] * e_ref[row + 1], pair_ref, 2)

    rows_loop(1, half + 2 * cbase - 1, source)

    v_refs = (v0, v1, v2, v3, v4, v5)
    level_setup(1, half + 2 * cbase - 1, 4, STEP_SCALE / 16.0, cg, ca, cwx, cwy, cwz, cinv, cd)
    level_sweeps(cbase, half, 0, COARSE_DEGREE, COARSE_LOW, False, 4, cb, cinv, cwx, cwy, cwz, ce, v_refs)
    total = v0[cbase : cbase + half, :cny]
    for v_ref in v_refs[1:]:
        total = total + v_ref[cbase : cbase + half, :cny]
    coarse_out[...] = compact(total.reshape(half * cny, nz), 4).reshape(half, cny, nz // 4)


def call(kernel, ins, outs, scratch):
    whole = pl.BlockSpec(memory_space=pltpu.VMEM)
    return pl.pallas_call(
        kernel,
        out_shape=[jax.ShapeDtypeStruct(shape, jnp.float32) for shape in outs],
        in_specs=[whole] * len(ins),
        out_specs=[whole] * len(outs),
        scratch_shapes=[pltpu.VMEM(shape, jnp.float32) for shape in scratch],
        compiler_params=pltpu.CompilerParams(vmem_limit_bytes=VMEM_BYTES),
    )(*ins)


def body(source, conductivity, absorption, brick_mask):
    doms, grps = lax.axis_size("dom"), lax.axis_size("grp")
    slots = min(grps - 1, 2)
    nx, ny, nz = source.shape
    lower, upper = DEGREE, DEGREE + 1

    def pairing(first):
        pairs = [(i, i + 1) for i in range(first, doms - 1, 2)]
        return pairs + [(j, i) for i, j in pairs]

    def swap_even(array):
        return lax.ppermute(array, "dom", pairing(0))

    def swap_odd(array):
        return lax.ppermute(array, "dom", pairing(1))

    downward = [(i + 1, i) for i in range(grps - 1)]
    upward = [(i, i + 1) for i in range(grps - 1)]

    def along_grp(arrays):
        if slots == 0:
            return []
        if slots == 1:
            return [lax.ppermute(arrays[0], "grp", downward + upward)]
        return [lax.ppermute(arrays[0], "grp", downward), lax.ppermute(arrays[-1], "grp", upward)]

    payload = (2 * lower + upper, ny, nz)
    packed = nx // 4
    outs = [source.shape, payload, payload, (2, packed, ny // 2, nz)] + [(3, nx, TILE, nz)] * slots
    g, to_even, to_odd, coeffs, *edges = call(
        functools.partial(pack_kernel, slots),
        (source, conductivity, absorption, brick_mask),
        outs,
        [(2, ny, nz)],
    )
    from_even, from_odd = swap_even(to_even), swap_odd(to_odd)
    beside = along_grp(edges)
    beside_even, beside_odd = along_grp([from_even]), along_grp([from_odd])
    coeff_parts = [coeffs, swap_even(coeffs), swap_odd(coeffs)]

    wide = (nx + 2 * upper, ny + slots * TILE, nz)
    fine_iterate, fine_residual, mid_source = call(
        functools.partial(fine_kernel, slots),
        (source, absorption, g, from_even, from_odd, *beside, *beside_even, *beside_odd),
        [source.shape, source.shape, (packed, ny // 2, nz)],
        [wide] * 13 + [(2, ny, nz)],
    )

    source_parts = [mid_source, swap_even(mid_source), swap_odd(mid_source)]
    q_ins, s_ins = [], []
    for q_part, s_part in zip(coeff_parts, source_parts):
        q_ins += [q_part] + along_grp([q_part])
        s_ins += [s_part] + along_grp([s_part])
    mid_y = (1 + slots) * ny // 2
    mid_wide = (3 * nx // 2, mid_y, nz)
    coarse_wide = (nx // 4 + 2 * COARSE_DEGREE, mid_y // 2, nz)
    mid_iterate, coarse_iterate = call(
        functools.partial(coarse_kernel, slots),
        (*q_ins, *s_ins),
        [(nx // 2, ny // 2, nz // 2), (nx // 4, ny // 4, nz // 4)],
        [mid_wide] * 13 + [coarse_wide] * 15 + [(mid_y, nz)],
    )
    return (fine_iterate, fine_residual, mid_iterate, coarse_iterate)


def solution(mesh):
    spec = P("dom", "grp", None)
    return jax.shard_map(body, mesh=mesh, in_specs=(spec,) * 4, out_specs=(spec,) * 4, check_vma=False)
```

```python
import functools

import jax
import jax.numpy as jnp
from jax import lax
from jax.experimental import pallas as pl
from jax.experimental.pallas import tpu as pltpu
from jax.sharding import PartitionSpec as P

DEGREE = 4
COARSE_DEGREE = 6

STEP_SCALE = 4.0
SMOOTH_LOW = 0.3
SMOOTH_HIGH = 2.0
COARSE_LOW = 0.05

BRICK = 8
TILE = 8
VMEM_BYTES = 48 * 1024 * 1024


def chebyshev_constants(degree, lowest, highest):
    middle = (highest + lowest) / 2.0
    spread = (highest - lowest) / 2.0
    relative = middle / spread
    previous = 1.0 / relative
    steps = []
    for _ in range(degree - 1):
        following = 1.0 / (2.0 * relative - previous)
        steps.append((following * previous, 2.0 * following / spread))
        previous = following
    return 1.0 / middle, steps


def lane_index(shape):
    return lax.broadcasted_iota(jnp.int32, shape, len(shape) - 1)


def ahead(value, axis, step=1):
    return pltpu.roll(value, value.shape[axis] - step, axis)


def behind(value, axis, step=1):
    return pltpu.roll(value, step, axis)


def positive(value):
    return jnp.where(value > 0.0, 1.0, 0.0)


def rows_loop(start, stop, body, block=14):
    count = stop - start
    if count <= 0:
        return
    loops = -(-count // block)
    size = count // loops

    def run(j, carry):
        for t in range(size):
            body(start + j * size + t)
        return carry

    if loops > 1:
        lax.fori_loop(0, loops, run, 0)
    else:
        run(0, 0)
    for i in range(start + loops * size, stop):
        body(i)


def level_setup(lo, hi, zstep, factor, g_ref, a_ref, wx_ref, wy_ref, wz_ref, inv_ref, d_ref):
    half = 0.5 * factor

    def weight_x(i):
        here, there = g_ref[i], g_ref[i + 1]
        wx_ref[i] = jnp.where((here > 0.0) & (there > 0.0), half * (here + there), 0.0)

    weight_x(lo - 1)

    def row(i):
        weight_x(i)
        here = g_ref[i]
        lanes = lane_index(here.shape)
        inside = here > 0.0
        there_y = ahead(here, 0)
        there_z = ahead(here, 1, zstep)
        wy = jnp.where(inside & (there_y > 0.0), half * (here + there_y), 0.0)
        wz = jnp.where(inside & (there_z > 0.0) & (lanes < here.shape[1] - zstep), half * (here + there_z), 0.0)
        wy_ref[i] = wy
        wz_ref[i] = wz
        faces = [wx_ref[i], wx_ref[i - 1], wy, behind(wy, 0), wz, behind(wz, 1, zstep)]
        wall = factor * a_ref[i]
        diagonal = 1.0 + jnp.where(faces[0] > 0.0, faces[0], wall)
        for face in faces[1:]:
            diagonal = diagonal + jnp.where(face > 0.0, face, wall)
        d_ref[i] = diagonal
        inv_ref[i] = jnp.where(inside, 1.0 / diagonal, 0.0)

    rows_loop(lo, hi, row)


def level_start(lo, hi, lowest, b_ref, inv_ref, e_ref, u_ref):
    first, _ = chebyshev_constants(1, lowest, SMOOTH_HIGH)

    def row(i):
        e = inv_ref[i] * b_ref[i]
        e_ref[i] = e
        u_ref[i] = e * first

    rows_loop(lo, hi, row)


def level_pass(lo, hi, k, degree, lowest, zstep, inv_ref, wx_ref, wy_ref, wz_ref, e_ref, u_refs):
    _, steps = chebyshev_constants(degree, lowest, SMOOTH_HIGH)
    old = u_refs[k]

    def row(i):
        u = old[i]
        wy = wy_ref[i]
        wz = wz_ref[i]
        coupled = wx_ref[i] * old[i + 1] + wx_ref[i - 1] * old[i - 1]
        coupled = coupled + (wy * ahead(u, 0) + behind(wy * u, 0))
        coupled = coupled + (wz * ahead(u, 1, zstep) + behind(wz * u, 1, zstep))
        e = e_ref[i] - u + inv_ref[i] * coupled
        e_ref[i] = e
        if k + 1 < degree:
            u_refs[k + 1][i] = steps[k][0] * u + steps[k][1] * e

    rows_loop(lo, hi, row)


def level_sweeps(base, size, reach, degree, lowest, keep, zstep, b_ref, inv_ref, wx_ref, wy_ref, wz_ref, e_ref, u_refs):
    passes = degree if keep else degree - 1
    width = reach + passes
    level_start(base - width, base + size + width, lowest, b_ref, inv_ref, e_ref, u_refs[0])
    for k in range(passes):
        width = reach + passes - 1 - k
        level_pass(
            base - width, base + size + width, k, degree, lowest, zstep, inv_ref, wx_ref, wy_ref, wz_ref, e_ref, u_refs
        )


def coarsen_rows(one, two, pair_ref, zstep):
    pair_ref[...] = one + two
    half = pair_ref.shape[0] // 2
    summed = pair_ref[pl.ds(0, half, 2), :] + pair_ref[pl.ds(1, half, 2), :]
    return (summed + ahead(summed, 1, zstep)) * 0.125


def pack_two(one, two):
    return jnp.where(lane_index(one.shape) % 2 == 0, one, behind(two, 1))


def unpack_two(packed):
    even = lane_index(packed.shape) % 2 == 0
    return jnp.where(even, packed, 0.0), jnp.where(even, ahead(packed, 1), 0.0)


def spread_mask(lines, spread, ny):
    wide = jnp.dot(lines.astype(jnp.float32), spread, preferred_element_type=jnp.float32)
    tiles = [jnp.broadcast_to(wide[by : by + 1], (BRICK, wide.shape[1])) for by in range(ny // BRICK)]
    return jnp.concatenate(tiles, axis=0)


def spread_matrix(nbz, nz):
    shape = (nbz, nz)
    column, line = lax.broadcasted_iota(jnp.int32, shape, 1), lax.broadcasted_iota(jnp.int32, shape, 0)
    return jnp.where(column // BRICK == line, 1.0, 0.0)


def start_all(copies, sems):
    started = [pltpu.make_async_copy(src, dst, sems.at[n]) for n, (src, dst) in enumerate(copies)]
    for copy in started:
        copy.start()
    return started


def edge_kernel(src_hbm, kap_hbm, ab_hbm, brick_hbm, a_out, b_out, bricks, sems):
    nx, ny, nz = src_hbm.shape
    lower, upper = DEGREE, DEGREE + 1
    even = lax.axis_index("dom") % 2 == 0
    copies = [(brick_hbm, bricks)]
    ups = (even, jnp.logical_not(even))
    for out, up in zip((a_out, b_out), ups):
        four = pl.ds(jnp.where(up, nx - lower, 0), lower)
        five = pl.ds(jnp.where(up, nx - upper, 0), upper)
        copies += [
            (kap_hbm.at[five], out.at[pl.ds(2 * lower, upper)]),
            (src_hbm.at[four], out.at[pl.ds(0, lower)]),
            (ab_hbm.at[four], out.at[pl.ds(lower, lower)]),
        ]
    started = start_all(copies, sems)
    for copy in started:
        copy.wait()
    nbx, _, nbz = bricks.shape
    spread = spread_matrix(nbz, nz)
    for out, up in zip((a_out, b_out), ups):
        mask = spread_mask(bricks[jnp.where(up, nbx - 1, 0)], spread, ny)
        for j in range(upper):
            out[2 * lower + j] = out[2 * lower + j] * mask


def block_kernel(slots, src_hbm, kap_hbm, ab_hbm, brick_hbm, _, b_ref, a_ref, g_ref, q_ref, *rest):
    y_outs, (bricks, pair_ref, sems) = rest[:slots], rest[slots:]
    nx, ny, nz = src_hbm.shape
    started = start_all([(brick_hbm, bricks), (kap_hbm, g_ref), (ab_hbm, a_ref), (src_hbm, b_ref)], sems)
    spread = spread_matrix(bricks.shape[2], nz)
    started[0].wait()
    started[1].wait()
    for bx in range(nx // BRICK):
        mask = spread_mask(bricks[bx], spread, ny)
        for x in range(bx * BRICK, (bx + 1) * BRICK):
            g_ref[x] = g_ref[x] * mask

    def packed_rows(field, ref):
        for j in range(nx // 4):
            cells = []
            for t in range(2):
                x = 4 * j + 2 * t
                scratch = pair_ref.at[(field * (nx // 4) + j) * 2 + t]
                cells.append(coarsen_rows(ref[x], ref[x + 1], scratch, 1))
            q_ref[field, j] = pack_two(*cells)

    packed_rows(0, g_ref)
    started[2].wait()
    packed_rows(1, a_ref)
    started[3].wait()

    for slot, out in enumerate(y_outs):
        at = pl.multiple_of(jnp.where(sends_up(slots, slot), ny - TILE, 0), TILE)
        for x in range(nx):
            out[0, x] = b_ref[x, pl.ds(at, TILE), :]
            out[1, x] = a_ref[x, pl.ds(at, TILE), :]
            out[2, x] = g_ref[x, pl.ds(at, TILE), :]


def sends_up(slots, slot):
    return lax.axis_index("grp") == 0 if slots == 1 else slot == 1


def slot_is_upper(slots, slot):
    return lax.axis_index("grp") == 0 if slots == 1 else slot == 0


def keep_near(value, is_upper, reach):
    rows = lax.broadcasted_iota(jnp.int32, value.shape, 0)
    size = value.shape[0]
    low = jnp.where(is_upper, 0, size - reach)
    high = jnp.where(is_upper, reach, size)
    return jnp.where((rows >= low) & (rows < high), value, 0.0)


def pack_rows(j, row, pair_ref):
    cells = []
    for t in range(2):
        x = 4 * j + 2 * t
        cells.append(coarsen_rows(row(x), row(x + 1), pair_ref.at[2 * j + t], 1))
    return pack_two(*cells)


def inner_packs(nx):
    first = -(-(DEGREE + 1) // 4)
    return range(first, nx // 4 - first)


class Joined:
    def __init__(self, own_ref, y_refs, field):
        self.own_ref, self.y_refs, self.field = own_ref, y_refs, field

    def __getitem__(self, x):
        parts = [self.own_ref[x]]
        for slot, y_ref in enumerate(self.y_refs):
            tile = y_ref[self.field, x]
            if self.field == 2:
                tile = keep_near(tile, slot_is_upper(len(self.y_refs), slot), DEGREE + 1)
            parts.append(tile)
        return jnp.concatenate(parts, axis=0)


class Rim:
    def __init__(self, nx, new_ref, before=None):
        self.nx, self.new_ref, self.before, self.written = nx, new_ref, before, set()

    def place(self, x):
        rows = self.new_ref.shape[0]
        return x + DEGREE + 1 if x < self.nx // 2 else rows - (self.nx + DEGREE + 1) + x

    def __getitem__(self, x):
        return self.new_ref[self.place(x)] if x in self.written else self.before[x]

    def __setitem__(self, x, value):
        self.new_ref[self.place(x)] = value
        self.written.add(x)


def inner_kernel(slots, *refs):
    b_in, a_in, g_in = refs[:3]
    y_refs = refs[3 : 3 + slots]
    wx, wy, wz, inv, d_ref, e_ref, u0, u1, u2, u3, it_out, res_out, s_ref, pair_ref = refs[3 + slots :]
    nx, ny, _ = b_in.shape
    b_ref, a_ref, g_ref = (Joined(ref, y_refs, field) for field, ref in enumerate((b_in, a_in, g_in)))
    u_refs = (u0, u1, u2, u3)
    level_setup(1, nx - 1, 1, STEP_SCALE, g_ref, a_ref, wx, wy, wz, inv, d_ref)
    level_start(1, nx - 1, SMOOTH_LOW, b_ref, inv, e_ref, u0)
    for k in range(DEGREE):
        level_pass(2 + k, nx - 2 - k, k, DEGREE, SMOOTH_LOW, 1, inv, wx, wy, wz, e_ref, u_refs)

    def finish(x):
        it_out[x] = (u0[x, :ny] + u1[x, :ny]) + (u2[x, :ny] + u3[x, :ny])
        res_out[x] = d_ref[x, :ny] * e_ref[x, :ny]

    rows_loop(DEGREE + 1, nx - DEGREE - 1, finish)
    for j in inner_packs(nx):
        s_ref[j] = pack_rows(j, lambda x: res_out[x], pair_ref)


def corner_kernel(slots, ra_ref, rb_ref, _, *outs):
    rows, ny, _ = ra_ref.shape
    for slot, out in enumerate(outs):
        at = pl.multiple_of(jnp.where(sends_up(slots, slot), ny - TILE, 0), TILE)
        for j in range(rows):
            out[0, j] = ra_ref[j, pl.ds(at, TILE), :]
            out[1, j] = rb_ref[j, pl.ds(at, TILE), :]


def gather_kernel(a_ref, b_ref, *refs):
    out = refs[-1]
    for j in range(a_ref.shape[0]):
        out[0, j] = a_ref[j]
        out[1, j] = b_ref[j]


def rim_kernel(slots, *refs):
    b_in, a_in, g_in = refs[:3]
    y_refs = refs[3 : 3 + slots]
    before, refs = refs[3 + slots : 13 + slots], refs[13 + slots :]
    res_in, s_in, ra_ref, rb_ref = refs[:4]
    c_refs = refs[4 : 4 + slots]
    it_out, res_out, s_ref = refs[4 + slots : 7 + slots]
    scratch, pair_ref = refs[7 + slots : -1], refs[-1]
    nx, ny, _ = b_in.shape
    lower, upper = DEGREE, DEGREE + 1

    b_ref, a_ref, g_ref = (
        Rim(nx, scratch[field], Joined(ref, y_refs, field)) for field, ref in enumerate((b_in, a_in, g_in))
    )
    wx, wy, wz, inv, d_ref, e_ref, *u_refs = (Rim(nx, new, old) for new, old in zip(scratch[3:], before))

    even = lax.axis_index("dom") % 2 == 0

    def received(j, is_above):
        from_even = even if is_above else jnp.logical_not(even)
        parts = [jnp.where(from_even, ra_ref[j], rb_ref[j])]
        for slot in range(slots):
            is_upper = slot_is_upper(slots, slot)
            tile = jnp.where(from_even, c_refs[slot][0, j], c_refs[slot][1, j])
            if j >= 2 * lower:
                tile = keep_near(tile, is_upper, upper)
            parts.append(tile)
        return jnp.concatenate(parts, axis=0)

    for is_above in (False, True):
        for j in range(lower):
            x = nx + j if is_above else j - lower
            b_ref[x] = received(j, is_above)
            a_ref[x] = received(lower + j, is_above)
        for j in range(upper):
            x = nx + j if is_above else j - upper
            g_ref[x] = received(2 * lower + j, is_above)

    for lo, hi in ((-lower, 1), (nx - 1, nx + lower)):
        level_setup(lo, hi, 1, STEP_SCALE, g_ref, a_ref, wx, wy, wz, inv, d_ref)
        level_start(lo, hi, SMOOTH_LOW, b_ref, inv, e_ref, u_refs[0])
    for k in range(DEGREE):
        out = DEGREE - 1 - k
        for lo, hi in ((-out, 2 + k), (nx - 2 - k, nx + out)):
            level_pass(lo, hi, k, DEGREE, SMOOTH_LOW, 1, inv, wx, wy, wz, e_ref, u_refs)

    place = {x: x for x in range(upper)}
    place.update({nx - upper + x: upper + x for x in range(upper)})
    for x, at in place.items():
        total = [u_ref[x][:ny] for u_ref in u_refs]
        it_out[at] = (total[0] + total[1]) + (total[2] + total[3])
        res_out[at] = d_ref[x][:ny] * e_ref[x][:ny]
    inner = inner_packs(nx)
    for j in range(nx // 4):
        if j in inner:
            s_ref[j] = s_in[j]
        else:
            s_ref[j] = pack_rows(j, lambda x: res_out[place[x]] if x in place else res_in[x], pair_ref)


def output_kernel(it_in, res_in, it_rim, res_rim, it_out, res_out, done_ref, sems):
    done_ref[...] = jnp.zeros_like(done_ref)
    nx = it_in.shape[0]
    rim = DEGREE + 1
    copies = []
    for inside, near, out in ((it_in, it_rim, it_out), (res_in, res_rim, res_out)):
        middle = pl.ds(rim, nx - 2 * rim)
        copies += [
            (inside.at[middle], out.at[middle]),
            (near.at[pl.ds(0, rim)], out.at[pl.ds(0, rim)]),
            (near.at[pl.ds(rim, rim)], out.at[pl.ds(nx - rim, rim)]),
        ]
    for copy in start_all(copies, sems):
        copy.wait()


def compact(value, step):
    nz = value.shape[-1]
    shape = (nz, nz // step)
    pick = jnp.where(
        lax.broadcasted_iota(jnp.int32, shape, 0) == step * lax.broadcasted_iota(jnp.int32, shape, 1), 1.0, 0.0
    )
    return jnp.dot(value, pick, preferred_element_type=jnp.float32, precision=lax.Precision.HIGHEST)


def part_starts(nx):
    even = lax.axis_index("dom") % 2 == 0
    return [nx, jnp.where(even, 2 * nx, 0), jnp.where(even, 0, 2 * nx)]


def coefficient_kernel(slots, *refs):
    own_refs, around_refs, refs = refs[: 1 + slots], refs[1 + slots : 2 + 2 * slots], refs[2 + 2 * slots :]
    wx, wy, wz, inv, d_ref, cwx, cwy, cwz, cinv, a_ref, g_ref, ca, cg, cd, pair_ref = refs
    _, packed, ny, _ = own_refs[0].shape
    nx = 2 * packed
    base = nx

    for part, start in enumerate(part_starts(nx)):
        for slot in range(1 + slots):
            q_ref = around_refs[slot].at[part - 1] if part else own_refs[slot]
            at = slice(slot * ny, (slot + 1) * ny)
            for j in range(packed):
                g_rows, a_rows = unpack_two(q_ref[0, j]), unpack_two(q_ref[1, j])
                for t in range(2):
                    g_row = g_rows[t]
                    if slot:
                        g_row = keep_near(g_row, slot_is_upper(slots, slot - 1), ny - 1)
                    g_ref[start + 2 * j + t, at] = g_row
                    a_ref[start + 2 * j + t, at] = a_rows[t]

    width = 2 * (COARSE_DEGREE - 1) + DEGREE
    level_setup(base - width, base + nx + width, 2, STEP_SCALE / 4.0, g_ref, a_ref, wx, wy, wz, inv, d_ref)

    rows = cg.shape[0]
    offset = base - 2 * COARSE_DEGREE
    for i in range(rows):
        row = offset + 2 * i
        g0, g1 = g_ref[row], g_ref[row + 1]
        whole = coarsen_rows(positive(g0), positive(g1), pair_ref.at[3 * i], 2) > 0.75
        first = lane_index(whole.shape) % 4 == 0
        cg[i] = jnp.where(whole & first, coarsen_rows(g0, g1, pair_ref.at[3 * i + 1], 2), 0.0)
        ca[i] = coarsen_rows(a_ref[row], a_ref[row + 1], pair_ref.at[3 * i + 2], 2)
    level_setup(1, rows - 1, 4, STEP_SCALE / 16.0, cg, ca, cwx, cwy, cwz, cinv, cd)


def coarse_kernel(slots, *refs):
    own_refs, around_refs, refs = refs[: 1 + slots], refs[1 + slots : 2 + 2 * slots], refs[2 + 2 * slots :]
    wx, wy, wz, inv, d_ref, cwx, cwy, cwz, cinv, mid_out, coarse_out = refs[:11]
    b_ref, e_ref, u0, u1, u2, u3, cb, ce, v0, v1, v2, v3, v4, v5, pair_ref = refs[11:]
    packed, ny, nz = own_refs[0].shape
    nx = 2 * packed
    base = nx

    for part, start in enumerate(part_starts(nx)):
        for slot in range(1 + slots):
            s_ref = around_refs[slot].at[part - 1] if part else own_refs[slot]
            at = slice(slot * ny, (slot + 1) * ny)
            for j in range(packed):
                for t, b_row in enumerate(unpack_two(s_ref[j])):
                    b_ref[start + 2 * j + t, at] = b_row

    reach = 2 * (COARSE_DEGREE - 1)
    u_refs = (u0, u1, u2, u3)
    level_sweeps(base, nx, reach, DEGREE, SMOOTH_LOW, True, 2, b_ref, inv, wx, wy, wz, e_ref, u_refs)

    total = u0[base : base + nx, :ny]
    for u_ref in u_refs[1:]:
        total = total + u_ref[base : base + nx, :ny]
    mid_out[...] = compact(total.reshape(nx * ny, nz), 2).reshape(nx, ny, nz // 2)

    half, cny = nx // 2, ny // 2
    cbase = COARSE_DEGREE
    offset = base - 2 * cbase
    for i in range(1, half + 2 * cbase - 1):
        row = offset + 2 * i
        cb[i] = coarsen_rows(d_ref[row] * e_ref[row], d_ref[row + 1] * e_ref[row + 1], pair_ref.at[i], 2)

    v_refs = (v0, v1, v2, v3, v4, v5)
    level_sweeps(cbase, half, 0, COARSE_DEGREE, COARSE_LOW, False, 4, cb, cinv, cwx, cwy, cwz, ce, v_refs)
    total = v0[cbase : cbase + half, :cny]
    for v_ref in v_refs[1:]:
        total = total + v_ref[cbase : cbase + half, :cny]
    coarse_out[...] = compact(total.reshape(half * cny, nz), 4).reshape(half, cny, nz // 4)


def call(kernel, ins, outs, scratch=(), in_hbm=0, out_hbm=0):
    vmem, hbm = pl.BlockSpec(memory_space=pltpu.VMEM), pl.BlockSpec(memory_space=pltpu.HBM)
    return pl.pallas_call(
        kernel,
        out_shape=[jax.ShapeDtypeStruct(shape, jnp.float32) for shape in outs],
        in_specs=[hbm] * in_hbm + [vmem] * (len(ins) - in_hbm),
        out_specs=[hbm] * out_hbm + [vmem] * (len(outs) - out_hbm),
        scratch_shapes=[pltpu.VMEM(shape, jnp.float32) if isinstance(shape, tuple) else shape for shape in scratch],
        compiler_params=pltpu.CompilerParams(vmem_limit_bytes=VMEM_BYTES),
    )(*ins)


def body(source, conductivity, absorption, brick_mask):
    doms, grps = lax.axis_size("dom"), lax.axis_size("grp")
    slots = min(grps - 1, 2)
    nx, ny, nz = source.shape
    lower, upper = DEGREE, DEGREE + 1

    def pairing(first):
        pairs = [(i, i + 1) for i in range(first, doms - 1, 2)]
        return pairs + [(j, i) for i, j in pairs]

    def swap_even(array):
        return lax.ppermute(array, "dom", pairing(0))

    def swap_odd(array):
        return lax.ppermute(array, "dom", pairing(1))

    downward = [(i + 1, i) for i in range(grps - 1)]
    upward = [(i, i + 1) for i in range(grps - 1)]

    def along_grp(arrays):
        if slots == 0:
            return []
        if slots == 1:
            return [lax.ppermute(arrays[0], "grp", downward + upward)]
        return [lax.ppermute(arrays[0], "grp", downward), lax.ppermute(arrays[-1], "grp", upward)]

    fields = [pltpu.with_memory_space_constraint(x, pltpu.HBM) for x in (source, conductivity, absorption, brick_mask)]
    bricks = pltpu.VMEM(brick_mask.shape, brick_mask.dtype)
    payload = (2 * lower + upper, ny, nz)
    to_even, to_odd = call(
        edge_kernel, fields, [payload, payload], [bricks, pltpu.SemaphoreType.DMA((7,))], in_hbm=4
    )
    from_even, from_odd = swap_even(to_even), swap_odd(to_odd)

    packed = nx // 4
    small = (packed, ny // 2, nz)
    b_own, a_own, g_own, coeffs, *edges = call(
        functools.partial(block_kernel, slots),
        (*fields, to_even),
        [source.shape] * 3 + [(2, *small)] + [(3, nx, TILE, nz)] * slots,
        [bricks, (4 * packed, ny, nz), pltpu.SemaphoreType.DMA((4,))],
        in_hbm=4,
    )
    own = (b_own, a_own, g_own, *along_grp(edges))
    coeffs_beside = along_grp([coeffs])
    coeffs_even, coeffs_odd = swap_even(coeffs), swap_odd(coeffs)

    wide = (nx, ny + slots * TILE, nz)
    pairs = (nx // 2, ny, nz)
    *state, it_inner, res_inner, s_inner = call(
        functools.partial(inner_kernel, slots),
        own,
        [wide] * 10 + [source.shape, source.shape, small],
        [pairs],
    )
    corners = call(
        functools.partial(corner_kernel, slots),
        (from_even, from_odd, s_inner),
        [(2, payload[0], TILE, nz)] * slots,
    )
    corners_beside = along_grp(corners)
    (coeffs_around,) = call(gather_kernel, (coeffs_even, coeffs_odd, *corners_beside), [(2, 2, *small)])
    q_ins = [coeffs, *coeffs_beside, coeffs_around, *along_grp([coeffs_around])]
    rim = (2 * upper, ny, nz)
    near = (4 * upper + 2, ny + slots * TILE, nz)
    it_rim, res_rim, mid_source = call(
        functools.partial(rim_kernel, slots),
        (*own, *state, res_inner, s_inner, from_even, from_odd, *corners_beside),
        [rim, rim, small],
        [near] * 13 + [pairs],
    )
    fine_iterate, fine_residual, written = call(
        output_kernel,
        (it_inner, res_inner, it_rim, res_rim),
        [source.shape, source.shape, (TILE, nz)],
        [pltpu.SemaphoreType.DMA((6,))],
        out_hbm=2,
    )

    source_even, source_odd = swap_even(mid_source), swap_odd(mid_source)
    mid_y = (1 + slots) * ny // 2
    mid_wide = (3 * nx // 2, mid_y, nz)
    coarse_rows = nx // 4 + 2 * COARSE_DEGREE
    coarse_wide = (coarse_rows, mid_y // 2, nz)
    weights = call(
        functools.partial(coefficient_kernel, slots),
        q_ins,
        [mid_wide] * 5 + [coarse_wide] * 4,
        [mid_wide] * 2 + [coarse_wide] * 3 + [(3 * coarse_rows, mid_y, nz)],
    )
    (around,) = call(gather_kernel, (source_even, source_odd, weights[-1], written), [(2, *small)])
    s_ins = [mid_source, *along_grp([mid_source]), around, *along_grp([around])]
    mid_iterate, coarse_iterate = call(
        functools.partial(coarse_kernel, slots),
        (*s_ins, *weights),
        [(nx // 2, ny // 2, nz // 2), (nx // 4, ny // 4, nz // 4)],
        [mid_wide] * 6 + [coarse_wide] * 8 + [(coarse_rows, mid_y, nz)],
    )
    return (fine_iterate, fine_residual, mid_iterate, coarse_iterate)


def solution(mesh):
    spec = P("dom", "grp", None)
    return jax.shard_map(body, mesh=mesh, in_specs=(spec,) * 4, out_specs=(spec,) * 4, check_vma=False)
```

```python
import functools

import jax
import jax.numpy as jnp
from jax import lax
from jax.experimental import pallas as pl
from jax.experimental.pallas import tpu as pltpu
from jax.sharding import PartitionSpec as P

DEGREE = 4
COARSE_DEGREE = 6

STEP_SCALE = 4.0
SMOOTH_LOW = 0.3
SMOOTH_HIGH = 2.0
COARSE_LOW = 0.05

BRICK = 8
TILE = 8
VMEM_BYTES = 24 * 1024 * 1024


def chebyshev_constants(degree, lowest, highest):
    middle = (highest + lowest) / 2.0
    spread = (highest - lowest) / 2.0
    relative = middle / spread
    previous = 1.0 / relative
    steps = []
    for _ in range(degree - 1):
        following = 1.0 / (2.0 * relative - previous)
        steps.append((following * previous, 2.0 * following / spread))
        previous = following
    return 1.0 / middle, steps


def lane_index(shape):
    return lax.broadcasted_iota(jnp.int32, shape, len(shape) - 1)


def ahead(value, axis, step=1):
    return pltpu.roll(value, value.shape[axis] - step, axis)


def behind(value, axis, step=1):
    return pltpu.roll(value, step, axis)


def positive(value):
    return jnp.where(value > 0.0, 1.0, 0.0)


def rows_loop(start, stop, body, block=50):
    count = stop - start
    if count <= 0:
        return
    loops = -(-count // block)
    size = count // loops

    def run(j, carry):
        for t in range(size):
            body(start + j * size + t)
        return carry

    if loops > 1:
        lax.fori_loop(0, loops, run, 0)
    else:
        run(0, 0)
    for i in range(start + loops * size, stop):
        body(i)


def level_setup(lo, hi, zstep, factor, g_ref, a_ref, wx_ref, wy_ref, wz_ref, inv_ref, d_ref):
    half = 0.5 * factor

    def weight_x(i):
        here, there = g_ref[i], g_ref[i + 1]
        wx_ref[i] = jnp.where((here > 0.0) & (there > 0.0), half * (here + there), 0.0)

    weight_x(lo - 1)

    def row(i):
        weight_x(i)
        here = g_ref[i]
        lanes = lane_index(here.shape)
        inside = here > 0.0
        there_y = ahead(here, 0)
        there_z = ahead(here, 1, zstep)
        wy = jnp.where(inside & (there_y > 0.0), half * (here + there_y), 0.0)
        wz = jnp.where(inside & (there_z > 0.0) & (lanes < here.shape[1] - zstep), half * (here + there_z), 0.0)
        wy_ref[i] = wy
        wz_ref[i] = wz
        faces = [wx_ref[i], wx_ref[i - 1], wy, behind(wy, 0), wz, behind(wz, 1, zstep)]
        wall = factor * a_ref[i]
        diagonal = 1.0 + jnp.where(faces[0] > 0.0, faces[0], wall)
        for face in faces[1:]:
            diagonal = diagonal + jnp.where(face > 0.0, face, wall)
        d_ref[i] = diagonal
        inv_ref[i] = jnp.where(inside, 1.0 / diagonal, 0.0)

    rows_loop(lo, hi, row, block=15)


def level_start(lo, hi, lowest, b_ref, inv_ref, e_ref, u_ref):
    first, _ = chebyshev_constants(1, lowest, SMOOTH_HIGH)

    def row(i):
        e = inv_ref[i] * b_ref[i]
        e_ref[i] = e
        u_ref[i] = e * first

    rows_loop(lo, hi, row)


def level_pass(lo, hi, k, degree, lowest, zstep, inv_ref, wx_ref, wy_ref, wz_ref, e_ref, u_refs):
    _, steps = chebyshev_constants(degree, lowest, SMOOTH_HIGH)
    old = u_refs[k]

    def row(i):
        u = old[i]
        wy = wy_ref[i]
        wz = wz_ref[i]
        coupled = wx_ref[i] * old[i + 1] + wx_ref[i - 1] * old[i - 1]
        coupled = coupled + (wy * ahead(u, 0) + behind(wy * u, 0))
        coupled = coupled + (wz * ahead(u, 1, zstep) + behind(wz * u, 1, zstep))
        e = e_ref[i] - u + inv_ref[i] * coupled
        e_ref[i] = e
        if k + 1 < degree:
            u_refs[k + 1][i] = steps[k][0] * u + steps[k][1] * e

    rows_loop(lo, hi, row)


def level_sweeps(base, size, reach, degree, lowest, keep, zstep, b_ref, inv_ref, wx_ref, wy_ref, wz_ref, e_ref, u_refs):
    passes = degree if keep else degree - 1
    width = reach + passes
    level_start(base - width, base + size + width, lowest, b_ref, inv_ref, e_ref, u_refs[0])
    for k in range(passes):
        width = reach + passes - 1 - k
        level_pass(
            base - width, base + size + width, k, degree, lowest, zstep, inv_ref, wx_ref, wy_ref, wz_ref, e_ref, u_refs
        )


def coarsen_rows(one, two, pair_ref, zstep):
    pair_ref[...] = one + two
    half = pair_ref.shape[0] // 2
    summed = pair_ref[pl.ds(0, half, 2), :] + pair_ref[pl.ds(1, half, 2), :]
    return (summed + ahead(summed, 1, zstep)) * 0.125


def pack_two(one, two):
    return jnp.where(lane_index(one.shape) % 2 == 0, one, behind(two, 1))


def unpack_two(packed):
    even = lane_index(packed.shape) % 2 == 0
    return jnp.where(even, packed, 0.0), jnp.where(even, ahead(packed, 1), 0.0)


def spread_mask(lines, spread, ny):
    wide = jnp.dot(lines.astype(jnp.float32), spread, preferred_element_type=jnp.float32)
    tiles = [jnp.broadcast_to(wide[by : by + 1], (BRICK, wide.shape[1])) for by in range(ny // BRICK)]
    return jnp.concatenate(tiles, axis=0)


def spread_matrix(nbz, nz):
    shape = (nbz, nz)
    column, line = lax.broadcasted_iota(jnp.int32, shape, 1), lax.broadcasted_iota(jnp.int32, shape, 0)
    return jnp.where(column // BRICK == line, 1.0, 0.0)


def start_all(copies, sems):
    started = [pltpu.make_async_copy(src, dst, sems.at[n]) for n, (src, dst) in enumerate(copies)]
    for copy in started:
        copy.start()
    return started


def block_kernel(slots, src_hbm, kap_hbm, ab_hbm, brick_hbm, b_ref, a_ref, g_ref, to_even, to_odd, q_ref, *rest):
    y_outs, (bricks, pair_ref, sems) = rest[:slots], rest[slots:]
    nx, ny, nz = src_hbm.shape
    lower, upper = DEGREE, DEGREE + 1
    started = start_all([(brick_hbm, bricks), (kap_hbm, g_ref), (ab_hbm, a_ref), (src_hbm, b_ref)], sems)
    spread = spread_matrix(bricks.shape[2], nz)
    started[0].wait()
    started[1].wait()
    for bx in range(nx // BRICK):
        mask = spread_mask(bricks[bx], spread, ny)
        for x in range(bx * BRICK, (bx + 1) * BRICK):
            g_ref[x] = g_ref[x] * mask

    def packed_rows(field, ref):
        for j in range(nx // 4):
            cells = []
            for t in range(2):
                x = 4 * j + 2 * t
                scratch = pair_ref.at[(field * (nx // 4) + j) * 2 + t]
                cells.append(coarsen_rows(ref[x], ref[x + 1], scratch, 1))
            q_ref[field * (nx // 4) + j] = pack_two(*cells)

    packed_rows(0, g_ref)
    started[2].wait()
    packed_rows(1, a_ref)
    started[3].wait()

    even = lax.axis_index("dom") % 2 == 0
    for out, up in ((to_even, even), (to_odd, jnp.logical_not(even))):
        four = jnp.where(up, nx - lower, 0)
        five = jnp.where(up, nx - upper, 0)
        for j in range(lower):
            out[j] = b_ref[four + j]
            out[lower + j] = a_ref[four + j]
        for j in range(upper):
            out[2 * lower + j] = g_ref[five + j]

    for slot, out in enumerate(y_outs):
        at = pl.multiple_of(jnp.where(sends_up(slots, slot), ny - TILE, 0), TILE)
        for x in range(nx):
            out[0, x] = b_ref[x, pl.ds(at, TILE), :]
            out[1, x] = a_ref[x, pl.ds(at, TILE), :]
            out[2, x] = g_ref[x, pl.ds(at, TILE), :]


def sends_up(slots, slot):
    return lax.axis_index("grp") == 0 if slots == 1 else slot == 1


def slot_is_upper(slots, slot):
    return lax.axis_index("grp") == 0 if slots == 1 else slot == 0


def keep_near(value, is_upper, reach):
    rows = lax.broadcasted_iota(jnp.int32, value.shape, 0)
    size = value.shape[0]
    low = jnp.where(is_upper, 0, size - reach)
    high = jnp.where(is_upper, reach, size)
    return jnp.where((rows >= low) & (rows < high), value, 0.0)


def pack_rows(j, row, pair_ref):
    cells = []
    for t in range(2):
        x = 4 * j + 2 * t
        cells.append(coarsen_rows(row(x), row(x + 1), pair_ref.at[2 * j + t], 1))
    return pack_two(*cells)


def inner_packs(nx):
    first = -(-(DEGREE + 1) // 4)
    return range(first, nx // 4 - first)


class Joined:
    def __init__(self, own_ref, y_refs, field):
        self.own_ref, self.y_refs, self.field = own_ref, y_refs, field

    def __getitem__(self, x):
        parts = [self.own_ref[x]]
        for slot, y_ref in enumerate(self.y_refs):
            tile = y_ref[self.field, x]
            if self.field == 2:
                tile = keep_near(tile, slot_is_upper(len(self.y_refs), slot), DEGREE + 1)
            parts.append(tile)
        return jnp.concatenate(parts, axis=0)


class Rim:
    def __init__(self, nx, new_ref, before=None):
        self.nx, self.new_ref, self.before, self.written = nx, new_ref, before, set()

    def place(self, x):
        rows = self.new_ref.shape[0]
        return x + DEGREE + 1 if x < self.nx // 2 else rows - (self.nx + DEGREE + 1) + x

    def __getitem__(self, x):
        return self.new_ref[self.place(x)] if x in self.written else self.before[x]

    def __setitem__(self, x, value):
        self.new_ref[self.place(x)] = value
        self.written.add(x)


def inner_kernel(slots, *refs):
    b_in, a_in, g_in = refs[:3]
    y_refs = refs[3 : 3 + slots]
    wx, wy, wz, inv, d_ref, e_ref, u0, u1, u2, u3, it_out, res_out, s_ref, pair_ref = refs[3 + slots :]
    nx, ny, _ = b_in.shape
    b_ref, a_ref, g_ref = (Joined(ref, y_refs, field) for field, ref in enumerate((b_in, a_in, g_in)))
    u_refs = (u0, u1, u2, u3)
    level_setup(1, nx - 1, 1, STEP_SCALE, g_ref, a_ref, wx, wy, wz, inv, d_ref)
    level_start(1, nx - 1, SMOOTH_LOW, b_ref, inv, e_ref, u0)
    for k in range(DEGREE):
        level_pass(2 + k, nx - 2 - k, k, DEGREE, SMOOTH_LOW, 1, inv, wx, wy, wz, e_ref, u_refs)

    def finish(x):
        it_out[x] = (u0[x, :ny] + u1[x, :ny]) + (u2[x, :ny] + u3[x, :ny])
        res_out[x] = d_ref[x, :ny] * e_ref[x, :ny]

    rows_loop(DEGREE + 1, nx - DEGREE - 1, finish)
    for j in inner_packs(nx):
        s_ref[j] = pack_rows(j, lambda x: res_out[x], pair_ref)


def corner_kernel(slots, ra_ref, rb_ref, _, *outs):
    rows, ny, _ = ra_ref.shape
    for slot, out in enumerate(outs):
        at = pl.multiple_of(jnp.where(sends_up(slots, slot), ny - TILE, 0), TILE)
        for j in range(rows):
            out[0, j] = ra_ref[j, pl.ds(at, TILE), :]
            out[1, j] = rb_ref[j, pl.ds(at, TILE), :]


def stack_kernel(count, *refs):
    out = refs[-1]
    for part in range(count):
        for j in range(out.shape[1]):
            out[part, j] = refs[part][j]


def stack(arrays, *earlier):
    (out,) = call(
        functools.partial(stack_kernel, len(arrays)), (*arrays, *earlier), [(len(arrays), *arrays[0].shape)]
    )
    return out


def rim_kernel(slots, *refs):
    b_in, a_in, g_in = refs[:3]
    y_refs = refs[3 : 3 + slots]
    before, refs = refs[3 + slots : 13 + slots], refs[13 + slots :]
    res_in, s_in, ra_ref, rb_ref = refs[:4]
    c_refs = refs[4 : 4 + slots]
    it_out, res_out, s_ref = refs[4 + slots : 7 + slots]
    scratch, pair_ref = refs[7 + slots : -1], refs[-1]
    nx, ny, _ = b_in.shape
    lower, upper = DEGREE, DEGREE + 1

    b_ref, a_ref, g_ref = (
        Rim(nx, scratch[field], Joined(ref, y_refs, field)) for field, ref in enumerate((b_in, a_in, g_in))
    )
    wx, wy, wz, inv, d_ref, e_ref, *u_refs = (Rim(nx, new, old) for new, old in zip(scratch[3:], before))

    even = lax.axis_index("dom") % 2 == 0

    def received(j, is_above):
        from_even = even if is_above else jnp.logical_not(even)
        parts = [jnp.where(from_even, ra_ref[j], rb_ref[j])]
        for slot in range(slots):
            is_upper = slot_is_upper(slots, slot)
            tile = jnp.where(from_even, c_refs[slot][0, j], c_refs[slot][1, j])
            if j >= 2 * lower:
                tile = keep_near(tile, is_upper, upper)
            parts.append(tile)
        return jnp.concatenate(parts, axis=0)

    for is_above in (False, True):
        for j in range(lower):
            x = nx + j if is_above else j - lower
            b_ref[x] = received(j, is_above)
            a_ref[x] = received(lower + j, is_above)
        for j in range(upper):
            x = nx + j if is_above else j - upper
            g_ref[x] = received(2 * lower + j, is_above)

    for lo, hi in ((-lower, 1), (nx - 1, nx + lower)):
        level_setup(lo, hi, 1, STEP_SCALE, g_ref, a_ref, wx, wy, wz, inv, d_ref)
        level_start(lo, hi, SMOOTH_LOW, b_ref, inv, e_ref, u_refs[0])
    for k in range(DEGREE):
        out = DEGREE - 1 - k
        for lo, hi in ((-out, 2 + k), (nx - 2 - k, nx + out)):
            level_pass(lo, hi, k, DEGREE, SMOOTH_LOW, 1, inv, wx, wy, wz, e_ref, u_refs)

    place = {x: x for x in range(upper)}
    place.update({nx - upper + x: upper + x for x in range(upper)})
    for x, at in place.items():
        total = [u_ref[x][:ny] for u_ref in u_refs]
        it_out[at] = (total[0] + total[1]) + (total[2] + total[3])
        res_out[at] = d_ref[x][:ny] * e_ref[x][:ny]
    inner = inner_packs(nx)
    for j in range(nx // 4):
        if j in inner:
            s_ref[j] = s_in[j]
        else:
            s_ref[j] = pack_rows(j, lambda x: res_out[place[x]] if x in place else res_in[x], pair_ref)


def output_kernel(it_in, res_in, it_rim, res_rim, it_out, res_out, done_ref, sems):
    done_ref[...] = jnp.zeros_like(done_ref)
    nx = it_in.shape[0]
    rim = DEGREE + 1
    copies = []
    for inside, near, out in ((it_in, it_rim, it_out), (res_in, res_rim, res_out)):
        middle = pl.ds(rim, nx - 2 * rim)
        copies += [
            (inside.at[middle], out.at[middle]),
            (near.at[pl.ds(0, rim)], out.at[pl.ds(0, rim)]),
            (near.at[pl.ds(rim, rim)], out.at[pl.ds(nx - rim, rim)]),
        ]
    for copy in start_all(copies, sems):
        copy.wait()


def compact(value, step):
    nz = value.shape[-1]
    shape = (nz, nz // step)
    pick = jnp.where(
        lax.broadcasted_iota(jnp.int32, shape, 0) == step * lax.broadcasted_iota(jnp.int32, shape, 1), 1.0, 0.0
    )
    return jnp.dot(value, pick, preferred_element_type=jnp.float32, precision=lax.Precision.HIGHEST)


def placed_parts(slots, nx, own_refs, around_refs):
    parts = [(nx, slot, ref) for slot, ref in enumerate(own_refs)]
    if slots == 1:
        core = lax.axis_index("grp")
        for which, (ref, above) in enumerate(zip(around_refs, (core == 0, core == 1))):
            start = jnp.where(above, 2 * nx, 0)
            parts += [(start, 0, ref.at[1 - which]), (start, 1, ref.at[which])]
    else:
        even = lax.axis_index("dom") % 2 == 0
        for which, above in enumerate((even, jnp.logical_not(even))):
            start = jnp.where(above, 2 * nx, 0)
            parts += [(start, slot, ref.at[which]) for slot, ref in enumerate(around_refs)]
    return parts


def coefficient_kernel(slots, *refs):
    own_refs, around_refs, refs = refs[: 1 + slots], refs[1 + slots : 2 + 2 * slots], refs[2 + 2 * slots :]
    wx, wy, wz, inv, d_ref, cwx, cwy, cwz, cinv, a_ref, g_ref, ca, cg, cd, pair_ref = refs
    packed, ny = own_refs[0].shape[0] // 2, own_refs[0].shape[1]
    nx = 2 * packed
    base = nx

    for start, slot, q_ref in placed_parts(slots, nx, own_refs, around_refs):
        at = slice(slot * ny, (slot + 1) * ny)
        for j in range(packed):
            g_rows, a_rows = unpack_two(q_ref[j]), unpack_two(q_ref[packed + j])
            for t in range(2):
                g_row = g_rows[t]
                if slot:
                    g_row = keep_near(g_row, slot_is_upper(slots, slot - 1), ny - 1)
                g_ref[start + 2 * j + t, at] = g_row
                a_ref[start + 2 * j + t, at] = a_rows[t]

    width = 2 * (COARSE_DEGREE - 1) + DEGREE
    level_setup(base - width, base + nx + width, 2, STEP_SCALE / 4.0, g_ref, a_ref, wx, wy, wz, inv, d_ref)

    rows = cg.shape[0]
    offset = base - 2 * COARSE_DEGREE
    for i in range(rows):
        row = offset + 2 * i
        g0, g1 = g_ref[row], g_ref[row + 1]
        whole = coarsen_rows(positive(g0), positive(g1), pair_ref.at[3 * i], 2) > 0.75
        first = lane_index(whole.shape) % 4 == 0
        cg[i] = jnp.where(whole & first, coarsen_rows(g0, g1, pair_ref.at[3 * i + 1], 2), 0.0)
        ca[i] = coarsen_rows(a_ref[row], a_ref[row + 1], pair_ref.at[3 * i + 2], 2)
    level_setup(1, rows - 1, 4, STEP_SCALE / 16.0, cg, ca, cwx, cwy, cwz, cinv, cd)


def coarse_kernel(slots, *refs):
    own_refs, around_refs, refs = refs[: 1 + slots], refs[1 + slots : 2 + 2 * slots], refs[2 + 2 * slots :]
    wx, wy, wz, inv, d_ref, cwx, cwy, cwz, cinv, mid_out, coarse_out = refs[:11]
    b_ref, e_ref, u0, u1, u2, u3, cb, ce, v0, v1, v2, v3, v4, v5, pair_ref = refs[11:]
    packed, ny, nz = own_refs[0].shape
    nx = 2 * packed
    base = nx

    for start, slot, s_ref in placed_parts(slots, nx, own_refs, around_refs):
        at = slice(slot * ny, (slot + 1) * ny)
        for j in range(packed):
            for t, b_row in enumerate(unpack_two(s_ref[j])):
                b_ref[start + 2 * j + t, at] = b_row

    reach = 2 * (COARSE_DEGREE - 1)
    u_refs = (u0, u1, u2, u3)
    level_sweeps(base, nx, reach, DEGREE, SMOOTH_LOW, True, 2, b_ref, inv, wx, wy, wz, e_ref, u_refs)

    total = u0[base : base + nx, :ny]
    for u_ref in u_refs[1:]:
        total = total + u_ref[base : base + nx, :ny]
    mid_out[...] = compact(total.reshape(nx * ny, nz), 2).reshape(nx, ny, nz // 2)

    half, cny = nx // 2, ny // 2
    cbase = COARSE_DEGREE
    offset = base - 2 * cbase
    for i in range(1, half + 2 * cbase - 1):
        row = offset + 2 * i
        cb[i] = coarsen_rows(d_ref[row] * e_ref[row], d_ref[row + 1] * e_ref[row + 1], pair_ref.at[i], 2)

    v_refs = (v0, v1, v2, v3, v4, v5)
    level_sweeps(cbase, half, 0, COARSE_DEGREE, COARSE_LOW, False, 4, cb, cinv, cwx, cwy, cwz, ce, v_refs)
    total = v0[cbase : cbase + half, :cny]
    for v_ref in v_refs[1:]:
        total = total + v_ref[cbase : cbase + half, :cny]
    coarse_out[...] = compact(total.reshape(half * cny, nz), 4).reshape(half, cny, nz // 4)


def call(kernel, ins, outs, scratch=(), in_hbm=0, out_hbm=0):
    vmem, hbm = pl.BlockSpec(memory_space=pltpu.VMEM), pl.BlockSpec(memory_space=pltpu.HBM)
    return pl.pallas_call(
        kernel,
        out_shape=[jax.ShapeDtypeStruct(shape, jnp.float32) for shape in outs],
        in_specs=[hbm] * in_hbm + [vmem] * (len(ins) - in_hbm),
        out_specs=[hbm] * out_hbm + [vmem] * (len(outs) - out_hbm),
        scratch_shapes=[pltpu.VMEM(shape, jnp.float32) if isinstance(shape, tuple) else shape for shape in scratch],
        compiler_params=pltpu.CompilerParams(vmem_limit_bytes=VMEM_BYTES),
    )(*ins)


def body(source, conductivity, absorption, brick_mask):
    doms, grps = lax.axis_size("dom"), lax.axis_size("grp")
    slots = min(grps - 1, 2)
    nx, ny, nz = source.shape
    lower, upper = DEGREE, DEGREE + 1

    def pairing(first):
        pairs = [(i, i + 1) for i in range(first, doms - 1, 2)]
        return pairs + [(j, i) for i, j in pairs]

    def swap_even(array):
        return lax.ppermute(array, "dom", pairing(0))

    def swap_odd(array):
        return lax.ppermute(array, "dom", pairing(1))

    downward = [(i + 1, i) for i in range(grps - 1)]
    upward = [(i, i + 1) for i in range(grps - 1)]

    def along_grp(arrays):
        if slots == 0:
            return []
        if slots == 1:
            return [lax.ppermute(arrays[0], "grp", downward + upward)]
        return [lax.ppermute(arrays[0], "grp", downward), lax.ppermute(arrays[-1], "grp", upward)]

    crossing = []
    for i in range(doms - 1):
        crossing += [(i * grps, (i + 1) * grps + 1), ((i + 1) * grps + 1, i * grps)]

    def send_around(own, beside):
        if slots == 1:
            core = lax.axis_index("grp")
            both = stack([own, beside[0]])
            return [lax.ppermute(both, ("dom", "grp"), crossing)]
        return [swap_even(own), swap_odd(own)]

    def share_around(arrays, *earlier):
        both = stack(arrays, *earlier)
        both = both.reshape(2, *both.shape[-3:])
        return [both, *along_grp([both])]

    fields = [pltpu.with_memory_space_constraint(x, pltpu.HBM) for x in (source, conductivity, absorption, brick_mask)]
    bricks = pltpu.VMEM(brick_mask.shape, brick_mask.dtype)
    payload = (2 * lower + upper, ny, nz)
    packed = nx // 4
    small = (packed, ny // 2, nz)
    b_own, a_own, g_own, to_even, to_odd, coeffs, *edges = call(
        functools.partial(block_kernel, slots),
        fields,
        [source.shape] * 3 + [payload] * 2 + [(2 * packed, ny // 2, nz)] + [(3, nx, TILE, nz)] * slots,
        [bricks, (4 * packed, ny, nz), pltpu.SemaphoreType.DMA((4,))],
        in_hbm=4,
    )
    from_even, from_odd = swap_even(to_even), swap_odd(to_odd)
    own = (b_own, a_own, g_own, *along_grp(edges))
    coeffs_beside = along_grp([coeffs])
    coeffs_sent = send_around(coeffs, coeffs_beside)

    wide = (nx, ny + slots * TILE, nz)
    pairs = (nx // 2, ny, nz)
    *state, it_inner, res_inner, s_inner = call(
        functools.partial(inner_kernel, slots),
        own,
        [wide] * 10 + [source.shape, source.shape, small],
        [pairs],
    )
    corners = call(
        functools.partial(corner_kernel, slots),
        (from_even, from_odd, s_inner),
        [(2, payload[0], TILE, nz)] * slots,
    )
    corners_beside = along_grp(corners)
    rim = (2 * upper, ny, nz)
    near = (4 * upper + 2, ny + slots * TILE, nz)
    it_rim, res_rim, mid_source = call(
        functools.partial(rim_kernel, slots),
        (*own, *state, res_inner, s_inner, from_even, from_odd, *corners_beside),
        [rim, rim, small],
        [near] * 13 + [pairs],
    )
    fine_iterate, fine_residual, written = call(
        output_kernel,
        (it_inner, res_inner, it_rim, res_rim),
        [source.shape, source.shape, (TILE, nz)],
        [pltpu.SemaphoreType.DMA((6,))],
        out_hbm=2,
    )

    source_beside = along_grp([mid_source])
    source_sent = send_around(mid_source, source_beside)
    q_ins = [coeffs, *coeffs_beside, *share_around(coeffs_sent, mid_source)]
    mid_y = (1 + slots) * ny // 2
    mid_wide = (3 * nx // 2, mid_y, nz)
    coarse_rows = nx // 4 + 2 * COARSE_DEGREE
    coarse_wide = (coarse_rows, mid_y // 2, nz)
    weights = call(
        functools.partial(coefficient_kernel, slots),
        q_ins,
        [mid_wide] * 5 + [coarse_wide] * 4,
        [mid_wide] * 2 + [coarse_wide] * 3 + [(3 * coarse_rows, mid_y, nz)],
    )
    s_ins = [mid_source, *source_beside, *share_around(source_sent, weights[-1], written)]
    mid_iterate, coarse_iterate = call(
        functools.partial(coarse_kernel, slots),
        (*s_ins, *weights),
        [(nx // 2, ny // 2, nz // 2), (nx // 4, ny // 4, nz // 4)],
        [mid_wide] * 6 + [coarse_wide] * 8 + [(coarse_rows, mid_y, nz)],
    )
    return (fine_iterate, fine_residual, mid_iterate, coarse_iterate)


def solution(mesh):
    spec = P("dom", "grp", None)
    return jax.shard_map(body, mesh=mesh, in_specs=(spec,) * 4, out_specs=(spec,) * 4, check_vma=False)
```

```python
import functools

import jax
import jax.numpy as jnp
from jax import lax
from jax.experimental import pallas as pl
from jax.experimental.pallas import tpu as pltpu
from jax.sharding import PartitionSpec as P

DEGREE = 4
COARSE_DEGREE = 6

STEP_SCALE = 4.0
SMOOTH_LOW = 0.3
SMOOTH_HIGH = 2.0
COARSE_LOW = 0.05

BRICK = 8
TILE = 8
VMEM_BYTES = 24 * 1024 * 1024


def chebyshev_constants(degree, lowest, highest):
    middle = (highest + lowest) / 2.0
    spread = (highest - lowest) / 2.0
    relative = middle / spread
    previous = 1.0 / relative
    steps = []
    for _ in range(degree - 1):
        following = 1.0 / (2.0 * relative - previous)
        steps.append((following * previous, 2.0 * following / spread))
        previous = following
    return 1.0 / middle, steps


def lane_index(shape):
    return lax.broadcasted_iota(jnp.int32, shape, len(shape) - 1)


def ahead(value, axis, step=1):
    return pltpu.roll(value, value.shape[axis] - step, axis)


def behind(value, axis, step=1):
    return pltpu.roll(value, step, axis)


def positive(value):
    return jnp.where(value > 0.0, 1.0, 0.0)


def rows_loop(start, stop, body, block=50):
    count = stop - start
    if count <= 0:
        return
    loops = -(-count // block)
    size = count // loops

    def run(j, carry):
        for t in range(size):
            body(start + j * size + t)
        return carry

    if loops > 1:
        lax.fori_loop(0, loops, run, 0)
    else:
        run(0, 0)
    for i in range(start + loops * size, stop):
        body(i)


def next_row(value, following, packed):
    if not packed:
        return following
    return jnp.where((lane_index(value.shape) & 1) == 0, ahead(value, 1), behind(following, 1))


def previous_row(before, value, packed):
    if not packed:
        return before
    return jnp.where((lane_index(value.shape) & 1) == 0, ahead(before, 1), behind(value, 1))


def level_setup(lo, hi, zstep, factor, g_ref, a_ref, wx_ref, wy_ref, wz_ref, inv_ref, d_ref, packed=False, wb_ref=None):
    half = 0.5 * factor

    def weight_x(i):
        here = g_ref[i]
        there = next_row(here, g_ref[i + 1], packed)
        wx_ref[i] = jnp.where((here > 0.0) & (there > 0.0), half * (here + there), 0.0)

    weight_x(lo - 1)

    def row(i):
        weight_x(i)
        here = g_ref[i]
        lanes = lane_index(here.shape)
        inside = here > 0.0
        there_y = ahead(here, 0)
        there_z = ahead(here, 1, zstep)
        wy = jnp.where(inside & (there_y > 0.0), half * (here + there_y), 0.0)
        wz = jnp.where(inside & (there_z > 0.0) & (lanes < here.shape[1] - zstep), half * (here + there_z), 0.0)
        wy_ref[i] = wy
        wz_ref[i] = wz
        wx = wx_ref[i]
        wb = behind(wy, 0)
        if wb_ref is not None:
            wb_ref[i] = wb
        faces = [wx, previous_row(wx_ref[i - 1], wx, packed), wy, wb, wz, behind(wz, 1, zstep)]
        wall = factor * a_ref[i]
        diagonal = 1.0 + jnp.where(faces[0] > 0.0, faces[0], wall)
        for face in faces[1:]:
            diagonal = diagonal + jnp.where(face > 0.0, face, wall)
        d_ref[i] = diagonal
        inv_ref[i] = jnp.where(inside, 1.0 / diagonal, 0.0)

    rows_loop(lo, hi, row, block=15)


class Circular:
    def __init__(self, ref):
        self.ref, self.size = ref, ref.shape[1] - 2 * TILE

    def __getitem__(self, i):
        return self.ref[i, TILE : TILE + self.size]

    def __setitem__(self, i, value):
        self.ref[i, TILE : TILE + self.size] = value
        self.ref[i, :TILE] = value[self.size - TILE :]
        self.ref[i, TILE + self.size :] = value[:TILE]

    def shifted(self, i, step):
        return self.ref[i, TILE + step : TILE + step + self.size]


def level_start(lo, hi, lowest, b_ref, inv_ref, e_ref, u_ref):
    first, _ = chebyshev_constants(1, lowest, SMOOTH_HIGH)

    def row(i):
        e = inv_ref[i] * b_ref[i]
        e_ref[i] = e
        u_ref[i] = e * first

    rows_loop(lo, hi, row)


def level_pass(lo, hi, k, degree, lowest, zstep, inv_ref, wx_ref, wy_ref, wz_ref, e_ref, u_refs, packed=False, wb_ref=None):
    _, steps = chebyshev_constants(degree, lowest, SMOOTH_HIGH)
    old = u_refs[k]

    def row(i):
        u = old[i]
        wx = wx_ref[i]
        wy = wy_ref[i]
        wz = wz_ref[i]
        coupled = wx * next_row(u, old[i + 1], packed)
        coupled = coupled + previous_row(wx_ref[i - 1] * old[i - 1], wx * u if packed else None, packed)
        if wb_ref is None:
            coupled = coupled + (wy * ahead(u, 0) + behind(wy * u, 0))
        else:
            coupled = coupled + (wy * old.shifted(i, 1) + wb_ref[i] * old.shifted(i, -1))
        coupled = coupled + (wz * ahead(u, 1, zstep) + behind(wz * u, 1, zstep))
        e = e_ref[i] - u + inv_ref[i] * coupled
        e_ref[i] = e
        if k + 1 < degree:
            u_refs[k + 1][i] = steps[k][0] * u + steps[k][1] * e

    rows_loop(lo, hi, row)


def level_sweeps(
    base, size, reach, degree, lowest, keep, zstep, b_ref, inv_ref, wx_ref, wy_ref, wz_ref, e_ref, u_refs, packed=False, wb_ref=None
):
    passes = degree if keep else degree - 1
    per = 2 if packed else 1
    width = -(-(reach + passes) // per)
    level_start(base - width, base + size + width, lowest, b_ref, inv_ref, e_ref, u_refs[0])
    weights = (inv_ref, wx_ref, wy_ref, wz_ref)
    for k in range(passes):
        width = -(-(reach + passes - 1 - k) // per)
        level_pass(base - width, base + size + width, k, degree, lowest, zstep, *weights, e_ref, u_refs, packed, wb_ref)


def coarsen_rows(one, two, pair_ref, zstep):
    pair_ref[...] = one + two
    half = pair_ref.shape[0] // 2
    summed = pair_ref[pl.ds(0, half, 2), :] + pair_ref[pl.ds(1, half, 2), :]
    return (summed + ahead(summed, 1, zstep)) * 0.125


def pack_two(one, two):
    return jnp.where((lane_index(one.shape) & 1) == 0, one, behind(two, 1))


def coarsen_packed(value, pair_ref):
    pair_ref[...] = value
    half = pair_ref.shape[0] // 2
    summed = pair_ref[pl.ds(0, half, 2), :] + pair_ref[pl.ds(1, half, 2), :]
    summed = summed + ahead(summed, 1)
    return (summed + ahead(summed, 1, 2)) * 0.125


def spread_mask(lines, spread, ny):
    wide = jnp.dot(lines.astype(jnp.float32), spread, preferred_element_type=jnp.float32)
    tiles = [jnp.broadcast_to(wide[by : by + 1], (BRICK, wide.shape[1])) for by in range(ny // BRICK)]
    return jnp.concatenate(tiles, axis=0)


def spread_matrix(nbz, nz):
    shape = (nbz, nz)
    column, line = lax.broadcasted_iota(jnp.int32, shape, 1), lax.broadcasted_iota(jnp.int32, shape, 0)
    return jnp.where(column // BRICK == line, 1.0, 0.0)


def start_all(copies, sems):
    started = [pltpu.make_async_copy(src, dst, sems.at[n]) for n, (src, dst) in enumerate(copies)]
    for copy in started:
        copy.start()
    return started


def block_kernel(slots, src_hbm, kap_hbm, ab_hbm, brick_hbm, b_ref, a_ref, g_ref, to_even, to_odd, q_ref, *rest):
    y_outs, (bricks, pair_ref, sems) = rest[:slots], rest[slots:]
    nx, ny, nz = src_hbm.shape
    lower, upper = DEGREE, DEGREE + 1
    started = start_all([(brick_hbm, bricks), (kap_hbm, g_ref), (ab_hbm, a_ref), (src_hbm, b_ref)], sems)
    spread = spread_matrix(bricks.shape[2], nz)
    started[0].wait()
    started[1].wait()
    for bx in range(nx // BRICK):
        mask = spread_mask(bricks[bx], spread, ny)
        for x in range(bx * BRICK, (bx + 1) * BRICK):
            g_ref[x] = g_ref[x] * mask

    def packed_rows(field, ref):
        for j in range(nx // 4):
            cells = []
            for t in range(2):
                x = 4 * j + 2 * t
                scratch = pair_ref.at[(field * (nx // 4) + j) * 2 + t]
                cells.append(coarsen_rows(ref[x], ref[x + 1], scratch, 1))
            q_ref[field * (nx // 4) + j] = pack_two(*cells)

    packed_rows(0, g_ref)
    started[2].wait()
    packed_rows(1, a_ref)
    started[3].wait()

    even = lax.axis_index("dom") % 2 == 0
    for out, up in ((to_even, even), (to_odd, jnp.logical_not(even))):
        four = jnp.where(up, nx - lower, 0)
        five = jnp.where(up, nx - upper, 0)
        for j in range(lower):
            out[j] = b_ref[four + j]
            out[lower + j] = a_ref[four + j]
        for j in range(upper):
            out[2 * lower + j] = g_ref[five + j]

    for slot, out in enumerate(y_outs):
        at = pl.multiple_of(jnp.where(sends_up(slots, slot), ny - TILE, 0), TILE)
        for x in range(nx):
            out[0, x] = b_ref[x, pl.ds(at, TILE), :]
            out[1, x] = a_ref[x, pl.ds(at, TILE), :]
            out[2, x] = g_ref[x, pl.ds(at, TILE), :]


def sends_up(slots, slot):
    return lax.axis_index("grp") == 0 if slots == 1 else slot == 1


def slot_is_upper(slots, slot):
    return lax.axis_index("grp") == 0 if slots == 1 else slot == 0


def keep_near(value, is_upper, reach):
    rows = lax.broadcasted_iota(jnp.int32, value.shape, 0)
    size = value.shape[0]
    low = jnp.where(is_upper, 0, size - reach)
    high = jnp.where(is_upper, reach, size)
    return jnp.where((rows >= low) & (rows < high), value, 0.0)


def pack_rows(j, row, pair_ref):
    cells = []
    for t in range(2):
        x = 4 * j + 2 * t
        cells.append(coarsen_rows(row(x), row(x + 1), pair_ref.at[2 * j + t], 1))
    return pack_two(*cells)


def inner_packs(nx):
    first = -(-(DEGREE + 1) // 4)
    return range(first, nx // 4 - first)


class Joined:
    def __init__(self, own_ref, y_refs, field):
        self.own_ref, self.y_refs, self.field = own_ref, y_refs, field

    def __getitem__(self, x):
        parts = [self.own_ref[x]]
        for slot, y_ref in enumerate(self.y_refs):
            tile = y_ref[self.field, x]
            if self.field == 2:
                tile = keep_near(tile, slot_is_upper(len(self.y_refs), slot), DEGREE + 1)
            parts.append(tile)
        return jnp.concatenate(parts, axis=0)


class Rim:
    def __init__(self, nx, new_ref, before=None):
        self.nx, self.new_ref, self.before, self.written = nx, new_ref, before, set()

    def place(self, x):
        rows = self.new_ref.shape[0]
        return x + DEGREE + 1 if x < self.nx // 2 else rows - (self.nx + DEGREE + 1) + x

    def __getitem__(self, x):
        return self.new_ref[self.place(x)] if x in self.written else self.before[x]

    def __setitem__(self, x, value):
        self.new_ref[self.place(x)] = value
        self.written.add(x)


def inner_kernel(slots, *refs):
    b_in, a_in, g_in = refs[:3]
    y_refs = refs[3 : 3 + slots]
    wx, wy, wz, inv, d_ref, e_ref, u0, u1, u2, u3, it_out, res_out, s_ref, pair_ref = refs[3 + slots :]
    nx, ny, _ = b_in.shape
    b_ref, a_ref, g_ref = (Joined(ref, y_refs, field) for field, ref in enumerate((b_in, a_in, g_in)))
    u_refs = (u0, u1, u2, u3)
    level_setup(1, nx - 1, 1, STEP_SCALE, g_ref, a_ref, wx, wy, wz, inv, d_ref)
    level_start(1, nx - 1, SMOOTH_LOW, b_ref, inv, e_ref, u0)
    for k in range(DEGREE):
        level_pass(2 + k, nx - 2 - k, k, DEGREE, SMOOTH_LOW, 1, inv, wx, wy, wz, e_ref, u_refs)

    def finish(x):
        it_out[x] = (u0[x, :ny] + u1[x, :ny]) + (u2[x, :ny] + u3[x, :ny])
        res_out[x] = d_ref[x, :ny] * e_ref[x, :ny]

    rows_loop(DEGREE + 1, nx - DEGREE - 1, finish)
    for j in inner_packs(nx):
        s_ref[j] = pack_rows(j, lambda x: res_out[x], pair_ref)


def corner_kernel(slots, ra_ref, rb_ref, _, *outs):
    rows, ny, _ = ra_ref.shape
    for slot, out in enumerate(outs):
        at = pl.multiple_of(jnp.where(sends_up(slots, slot), ny - TILE, 0), TILE)
        for j in range(rows):
            out[0, j] = ra_ref[j, pl.ds(at, TILE), :]
            out[1, j] = rb_ref[j, pl.ds(at, TILE), :]


def stack_kernel(count, *refs):
    out = refs[-1]
    for part in range(count):
        for j in range(out.shape[1]):
            out[part, j] = refs[part][j]


def stack(arrays, *earlier):
    (out,) = call(
        functools.partial(stack_kernel, len(arrays)), (*arrays, *earlier), [(len(arrays), *arrays[0].shape)]
    )
    return out


def rim_kernel(slots, *refs):
    b_in, a_in, g_in = refs[:3]
    y_refs = refs[3 : 3 + slots]
    before, refs = refs[3 + slots : 13 + slots], refs[13 + slots :]
    res_in, s_in, ra_ref, rb_ref = refs[:4]
    c_refs = refs[4 : 4 + slots]
    it_out, res_out, s_ref = refs[4 + slots : 7 + slots]
    scratch, pair_ref = refs[7 + slots : -1], refs[-1]
    nx, ny, _ = b_in.shape
    lower, upper = DEGREE, DEGREE + 1

    b_ref, a_ref, g_ref = (
        Rim(nx, scratch[field], Joined(ref, y_refs, field)) for field, ref in enumerate((b_in, a_in, g_in))
    )
    wx, wy, wz, inv, d_ref, e_ref, *u_refs = (Rim(nx, new, old) for new, old in zip(scratch[3:], before))

    even = lax.axis_index("dom") % 2 == 0

    def received(j, is_above):
        from_even = even if is_above else jnp.logical_not(even)
        parts = [jnp.where(from_even, ra_ref[j], rb_ref[j])]
        for slot in range(slots):
            is_upper = slot_is_upper(slots, slot)
            tile = jnp.where(from_even, c_refs[slot][0, j], c_refs[slot][1, j])
            if j >= 2 * lower:
                tile = keep_near(tile, is_upper, upper)
            parts.append(tile)
        return jnp.concatenate(parts, axis=0)

    for is_above in (False, True):
        for j in range(lower):
            x = nx + j if is_above else j - lower
            b_ref[x] = received(j, is_above)
            a_ref[x] = received(lower + j, is_above)
        for j in range(upper):
            x = nx + j if is_above else j - upper
            g_ref[x] = received(2 * lower + j, is_above)

    for lo, hi in ((-lower, 1), (nx - 1, nx + lower)):
        level_setup(lo, hi, 1, STEP_SCALE, g_ref, a_ref, wx, wy, wz, inv, d_ref)
        level_start(lo, hi, SMOOTH_LOW, b_ref, inv, e_ref, u_refs[0])
    for k in range(DEGREE):
        out = DEGREE - 1 - k
        for lo, hi in ((-out, 2 + k), (nx - 2 - k, nx + out)):
            level_pass(lo, hi, k, DEGREE, SMOOTH_LOW, 1, inv, wx, wy, wz, e_ref, u_refs)

    place = {x: x for x in range(upper)}
    place.update({nx - upper + x: upper + x for x in range(upper)})
    for x, at in place.items():
        total = [u_ref[x][:ny] for u_ref in u_refs]
        it_out[at] = (total[0] + total[1]) + (total[2] + total[3])
        res_out[at] = d_ref[x][:ny] * e_ref[x][:ny]
    inner = inner_packs(nx)
    for j in range(nx // 4):
        if j in inner:
            s_ref[j] = s_in[j]
        else:
            s_ref[j] = pack_rows(j, lambda x: res_out[place[x]] if x in place else res_in[x], pair_ref)


def output_kernel(it_in, res_in, it_rim, res_rim, it_out, res_out, done_ref, sems):
    done_ref[...] = jnp.zeros_like(done_ref)
    nx = it_in.shape[0]
    rim = DEGREE + 1
    copies = []
    for inside, near, out in ((it_in, it_rim, it_out), (res_in, res_rim, res_out)):
        middle = pl.ds(rim, nx - 2 * rim)
        copies += [
            (inside.at[middle], out.at[middle]),
            (near.at[pl.ds(0, rim)], out.at[pl.ds(0, rim)]),
            (near.at[pl.ds(rim, rim)], out.at[pl.ds(nx - rim, rim)]),
        ]
    for copy in start_all(copies, sems):
        copy.wait()


def compact(value, step, first=0):
    nz = value.shape[-1]
    shape = (nz, nz // step)
    pick = jnp.where(
        lax.broadcasted_iota(jnp.int32, shape, 0) == first + step * lax.broadcasted_iota(jnp.int32, shape, 1), 1.0, 0.0
    )
    return jnp.dot(value, pick, preferred_element_type=jnp.float32, precision=lax.Precision.HIGHEST)


def placed_parts(slots, rows, own_refs, around_refs):
    parts = [(rows, slot, ref) for slot, ref in enumerate(own_refs)]
    if slots == 1:
        core = lax.axis_index("grp")
        for which, (ref, above) in enumerate(zip(around_refs, (core == 0, core == 1))):
            start = jnp.where(above, 2 * rows, 0)
            parts += [(start, 0, ref.at[1 - which]), (start, 1, ref.at[which])]
    else:
        even = lax.axis_index("dom") % 2 == 0
        for which, above in enumerate((even, jnp.logical_not(even))):
            start = jnp.where(above, 2 * rows, 0)
            parts += [(start, slot, ref.at[which]) for slot, ref in enumerate(around_refs)]
    return parts


def coefficient_kernel(slots, *refs):
    own_refs, around_refs, refs = refs[: 1 + slots], refs[1 + slots : 2 + 2 * slots], refs[2 + 2 * slots :]
    wx, wy, wz, wb, inv, d_ref, cwx, cwy, cwz, cinv, a_ref, g_ref, ca, cg, cd, pair_ref = refs
    rows, ny = own_refs[0].shape[0] // 2, own_refs[0].shape[1]
    for start, slot, q_ref in placed_parts(slots, rows, own_refs, around_refs):
        at = slice(slot * ny, (slot + 1) * ny)
        for j in range(rows):
            g_row = q_ref[j]
            if slot:
                g_row = keep_near(g_row, slot_is_upper(slots, slot - 1), ny - 1)
            g_ref[start + j, at] = g_row
            a_ref[start + j, at] = q_ref[rows + j]

    width = -(-(2 * (COARSE_DEGREE - 1) + DEGREE) // 2)
    level_setup(rows - width, 2 * rows + width, 2, STEP_SCALE / 4.0, g_ref, a_ref, wx, wy, wz, inv, d_ref, True, wb)

    coarse_rows = cg.shape[0]
    def coefficients(i):
        row = rows - COARSE_DEGREE + i
        g = g_ref[row]
        whole = coarsen_packed(positive(g), pair_ref.at[3 * i]) > 0.75
        first = (lane_index(whole.shape) & 3) == 0
        cg[i] = jnp.where(whole & first, coarsen_packed(g, pair_ref.at[3 * i + 1]), 0.0)
        ca[i] = coarsen_packed(a_ref[row], pair_ref.at[3 * i + 2])

    rows_loop(0, coarse_rows, coefficients, block=10)
    level_setup(1, coarse_rows - 1, 4, STEP_SCALE / 16.0, cg, ca, cwx, cwy, cwz, cinv, cd)


def coarse_kernel(slots, *refs):
    own_refs, around_refs, refs = refs[: 1 + slots], refs[1 + slots : 2 + 2 * slots], refs[2 + 2 * slots :]
    wx, wy, wz, wb, inv, d_ref, cwx, cwy, cwz, cinv, mid_out, coarse_out = refs[:12]
    b_ref, e_ref, u0, u1, u2, u3, cb, ce, v0, v1, v2, v3, v4, v5, pair_ref = refs[12:]
    rows, ny, nz = own_refs[0].shape
    for start, slot, s_ref in placed_parts(slots, rows, own_refs, around_refs):
        at = slice(slot * ny, (slot + 1) * ny)
        for j in range(rows):
            b_ref[start + j, at] = s_ref[j]

    reach = 2 * (COARSE_DEGREE - 1)
    u_refs = (u0, u1, u2, u3)
    updates = [Circular(u_ref) for u_ref in u_refs]
    level_sweeps(rows, rows, reach, DEGREE, SMOOTH_LOW, True, 2, b_ref, inv, wx, wy, wz, e_ref, updates, True, wb)

    total = u0[rows : 2 * rows, TILE : TILE + ny]
    for u_ref in u_refs[1:]:
        total = total + u_ref[rows : 2 * rows, TILE : TILE + ny]
    total = total.reshape(rows * ny, nz)
    for t in range(2):
        lines = compact(total, 2, t).reshape(rows, ny, nz // 2)
        for j in range(rows):
            mid_out[2 * j + t] = lines[j]

    half, cny = rows, ny // 2
    cbase = COARSE_DEGREE
    def source(i):
        row = rows - cbase + i
        cb[i] = coarsen_packed(d_ref[row] * e_ref[row], pair_ref.at[i])

    rows_loop(1, half + 2 * cbase - 1, source)
    v_refs = (v0, v1, v2, v3, v4, v5)
    level_sweeps(cbase, half, 0, COARSE_DEGREE, COARSE_LOW, False, 4, cb, cinv, cwx, cwy, cwz, ce, v_refs)
    total = v0[cbase : cbase + half, :cny]
    for v_ref in v_refs[1:]:
        total = total + v_ref[cbase : cbase + half, :cny]
    coarse_out[...] = compact(total.reshape(half * cny, nz), 4).reshape(half, cny, nz // 4)


def call(kernel, ins, outs, scratch=(), in_hbm=0, out_hbm=0):
    vmem, hbm = pl.BlockSpec(memory_space=pltpu.VMEM), pl.BlockSpec(memory_space=pltpu.HBM)
    return pl.pallas_call(
        kernel,
        out_shape=[jax.ShapeDtypeStruct(shape, jnp.float32) for shape in outs],
        in_specs=[hbm] * in_hbm + [vmem] * (len(ins) - in_hbm),
        out_specs=[hbm] * out_hbm + [vmem] * (len(outs) - out_hbm),
        scratch_shapes=[pltpu.VMEM(shape, jnp.float32) if isinstance(shape, tuple) else shape for shape in scratch],
        compiler_params=pltpu.CompilerParams(vmem_limit_bytes=VMEM_BYTES),
    )(*ins)


def body(source, conductivity, absorption, brick_mask):
    doms, grps = lax.axis_size("dom"), lax.axis_size("grp")
    slots = min(grps - 1, 2)
    nx, ny, nz = source.shape
    lower, upper = DEGREE, DEGREE + 1

    def pairing(first):
        pairs = [(i, i + 1) for i in range(first, doms - 1, 2)]
        return pairs + [(j, i) for i, j in pairs]

    def swap_even(array):
        return lax.ppermute(array, "dom", pairing(0))

    def swap_odd(array):
        return lax.ppermute(array, "dom", pairing(1))

    downward = [(i + 1, i) for i in range(grps - 1)]
    upward = [(i, i + 1) for i in range(grps - 1)]

    def along_grp(arrays):
        if slots == 0:
            return []
        if slots == 1:
            return [lax.ppermute(arrays[0], "grp", downward + upward)]
        return [lax.ppermute(arrays[0], "grp", downward), lax.ppermute(arrays[-1], "grp", upward)]

    crossing = []
    for i in range(doms - 1):
        crossing += [(i * grps, (i + 1) * grps + 1), ((i + 1) * grps + 1, i * grps)]

    def send_around(own, beside):
        if slots == 1:
            both = stack([own, beside[0]])
            return [lax.ppermute(both, ("dom", "grp"), crossing)], both
        return [swap_even(own), swap_odd(own)], own

    def share_around(arrays, *earlier):
        both = stack(arrays, *earlier)
        both = both.reshape(2, *both.shape[-3:])
        return [both, *along_grp([both])]

    fields = [pltpu.with_memory_space_constraint(x, pltpu.HBM) for x in (source, conductivity, absorption, brick_mask)]
    bricks = pltpu.VMEM(brick_mask.shape, brick_mask.dtype)
    payload = (2 * lower + upper, ny, nz)
    packed = nx // 4
    small = (packed, ny // 2, nz)
    b_own, a_own, g_own, to_even, to_odd, coeffs, *edges = call(
        functools.partial(block_kernel, slots),
        fields,
        [source.shape] * 3 + [payload] * 2 + [(2 * packed, ny // 2, nz)] + [(3, nx, TILE, nz)] * slots,
        [bricks, (4 * packed, ny, nz), pltpu.SemaphoreType.DMA((4,))],
        in_hbm=4,
    )
    from_even, from_odd = swap_even(to_even), swap_odd(to_odd)
    own = (b_own, a_own, g_own, *along_grp(edges))
    coeffs_beside = along_grp([coeffs])
    coeffs_sent, _ = send_around(coeffs, coeffs_beside)

    wide = (nx, ny + slots * TILE, nz)
    pairs = (nx // 2, ny, nz)
    *state, it_inner, res_inner, s_inner = call(
        functools.partial(inner_kernel, slots),
        own,
        [wide] * 10 + [source.shape, source.shape, small],
        [pairs],
    )
    corners = call(
        functools.partial(corner_kernel, slots),
        (from_even, from_odd, s_inner),
        [(2, payload[0], TILE, nz)] * slots,
    )
    corners_beside = along_grp(corners)
    rim = (2 * upper, ny, nz)
    near = (4 * upper + 2, ny + slots * TILE, nz)
    it_rim, res_rim, mid_source = call(
        functools.partial(rim_kernel, slots),
        (*own, *state, res_inner, s_inner, from_even, from_odd, *corners_beside),
        [rim, rim, small],
        [near] * 13 + [pairs],
    )
    fine_iterate, fine_residual, written = call(
        output_kernel,
        (it_inner, res_inner, it_rim, res_rim),
        [source.shape, source.shape, (TILE, nz)],
        [pltpu.SemaphoreType.DMA((6,))],
        out_hbm=2,
    )

    source_beside = along_grp([mid_source])
    source_sent, sending = send_around(mid_source, source_beside)
    q_ins = [coeffs, *coeffs_beside, *share_around(coeffs_sent, sending)]
    mid_y = (1 + slots) * ny // 2
    mid_wide = (3 * packed, mid_y, nz)
    coarse_rows = nx // 4 + 2 * COARSE_DEGREE
    coarse_wide = (coarse_rows, mid_y // 2, nz)
    weights = call(
        functools.partial(coefficient_kernel, slots),
        q_ins,
        [mid_wide] * 6 + [coarse_wide] * 4,
        [mid_wide] * 2 + [coarse_wide] * 3 + [(3 * coarse_rows, mid_y, nz)],
    )
    s_ins = [mid_source, *source_beside, *share_around(source_sent, weights[-1], written)]
    mid_iterate, coarse_iterate = call(
        functools.partial(coarse_kernel, slots),
        (*s_ins, *weights),
        [(nx // 2, ny // 2, nz // 2), (nx // 4, ny // 4, nz // 4)],
        [mid_wide] * 2 + [(3 * packed, mid_y + 2 * TILE, nz)] * 4 + [coarse_wide] * 8 + [(coarse_rows, mid_y, nz)],
    )
    return (fine_iterate, fine_residual, mid_iterate, coarse_iterate)


def solution(mesh):
    spec = P("dom", "grp", None)
    return jax.shard_map(body, mesh=mesh, in_specs=(spec,) * 4, out_specs=(spec,) * 4, check_vma=False)
```

```python
import functools

import jax
import jax.numpy as jnp
from jax import lax
from jax.experimental import pallas as pl
from jax.experimental.pallas import tpu as pltpu
from jax.sharding import PartitionSpec as P

DEGREE = 4
COARSE_DEGREE = 6

STEP_SCALE = 4.0
SMOOTH_LOW = 0.3
SMOOTH_HIGH = 2.0
COARSE_LOW = 0.05

BRICK = 8
TILE = 8
VMEM_BYTES = 24 * 1024 * 1024


def chebyshev_constants(degree, lowest, highest):
    middle = (highest + lowest) / 2.0
    spread = (highest - lowest) / 2.0
    relative = middle / spread
    previous = 1.0 / relative
    steps = []
    for _ in range(degree - 1):
        following = 1.0 / (2.0 * relative - previous)
        steps.append((following * previous, 2.0 * following / spread))
        previous = following
    return 1.0 / middle, steps


def lane_index(shape):
    return lax.broadcasted_iota(jnp.int32, shape, len(shape) - 1)


def ahead(value, axis, step=1):
    return pltpu.roll(value, value.shape[axis] - step, axis)


def behind(value, axis, step=1):
    return pltpu.roll(value, step, axis)


def positive(value):
    return jnp.where(value > 0.0, 1.0, 0.0)


def rows_loop(start, stop, body, block=50):
    count = stop - start
    if count <= 0:
        return
    loops = -(-count // block)
    size = count // loops

    def run(j, carry):
        for t in range(size):
            body(start + j * size + t)
        return carry

    if loops > 1:
        lax.fori_loop(0, loops, run, 0)
    else:
        run(0, 0)
    for i in range(start + loops * size, stop):
        body(i)


def next_row(value, following, packed):
    if not packed:
        return following
    return jnp.where((lane_index(value.shape) & 1) == 0, ahead(value, 1), behind(following, 1))


def previous_row(before, value, packed):
    if not packed:
        return before
    return jnp.where((lane_index(value.shape) & 1) == 0, ahead(before, 1), behind(value, 1))


def level_setup(lo, hi, zstep, factor, g_ref, a_ref, wx_ref, wy_ref, wz_ref, inv_ref, d_ref, packed=False, wb_ref=None):
    half = 0.5 * factor

    def weight_x(i):
        here = g_ref[i]
        there = next_row(here, g_ref[i + 1], packed)
        wx_ref[i] = jnp.where((here > 0.0) & (there > 0.0), half * (here + there), 0.0)

    weight_x(lo - 1)

    def row(i):
        weight_x(i)
        here = g_ref[i]
        lanes = lane_index(here.shape)
        inside = here > 0.0
        there_y = ahead(here, 0)
        there_z = ahead(here, 1, zstep)
        wy = jnp.where(inside & (there_y > 0.0), half * (here + there_y), 0.0)
        wz = jnp.where(inside & (there_z > 0.0) & (lanes < here.shape[1] - zstep), half * (here + there_z), 0.0)
        wy_ref[i] = wy
        wz_ref[i] = wz
        wx = wx_ref[i]
        wb = behind(wy, 0)
        if wb_ref is not None:
            wb_ref[i] = wb
        faces = [wx, previous_row(wx_ref[i - 1], wx, packed), wy, wb, wz, behind(wz, 1, zstep)]
        wall = factor * a_ref[i]
        diagonal = 1.0 + jnp.where(faces[0] > 0.0, faces[0], wall)
        for face in faces[1:]:
            diagonal = diagonal + jnp.where(face > 0.0, face, wall)
        d_ref[i] = diagonal
        inv_ref[i] = jnp.where(inside, 1.0 / diagonal, 0.0)

    rows_loop(lo, hi, row, block=15)


class Circular:
    def __init__(self, ref):
        self.ref, self.size = ref, ref.shape[1] - 2 * TILE

    def __getitem__(self, i):
        return self.ref[i, TILE : TILE + self.size]

    def __setitem__(self, i, value):
        self.ref[i, TILE : TILE + self.size] = value
        self.ref[i, :TILE] = value[self.size - TILE :]
        self.ref[i, TILE + self.size :] = value[:TILE]

    def shifted(self, i, step):
        return self.ref[i, TILE + step : TILE + step + self.size]


def level_start(lo, hi, lowest, b_ref, inv_ref, e_ref, u_ref):
    first, _ = chebyshev_constants(1, lowest, SMOOTH_HIGH)

    def row(i):
        e = inv_ref[i] * b_ref[i]
        e_ref[i] = e
        u_ref[i] = e * first

    rows_loop(lo, hi, row)


def level_pass(lo, hi, k, degree, lowest, zstep, inv_ref, wx_ref, wy_ref, wz_ref, e_ref, u_refs, packed=False, wb_ref=None):
    _, steps = chebyshev_constants(degree, lowest, SMOOTH_HIGH)
    old = u_refs[k]
    kept = {}

    def row(i):
        if isinstance(i, int) and i - 1 in kept:
            u, before = kept.pop(i - 1)
        else:
            u, before = old[i], wx_ref[i - 1] * old[i - 1]
        following = old[i + 1]
        wx = wx_ref[i]
        wy = wy_ref[i]
        wz = wz_ref[i]
        weighted = wx * u
        if isinstance(i, int):
            kept[i] = following, weighted
        coupled = wx * next_row(u, following, packed) + previous_row(before, weighted, packed)
        if wb_ref is None:
            coupled = coupled + (wy * ahead(u, 0) + behind(wy * u, 0))
        else:
            coupled = coupled + (wy * old.shifted(i, 1) + wb_ref[i] * old.shifted(i, -1))
        coupled = coupled + (wz * ahead(u, 1, zstep) + behind(wz * u, 1, zstep))
        e = e_ref[i] - u + inv_ref[i] * coupled
        e_ref[i] = e
        if k + 1 < degree:
            u_refs[k + 1][i] = steps[k][0] * u + steps[k][1] * e

    rows_loop(lo, hi, row)


def level_sweeps(
    base, size, reach, degree, lowest, keep, zstep, b_ref, inv_ref, wx_ref, wy_ref, wz_ref, e_ref, u_refs, packed=False, wb_ref=None
):
    passes = degree if keep else degree - 1
    per = 2 if packed else 1
    width = -(-(reach + passes) // per)
    level_start(base - width, base + size + width, lowest, b_ref, inv_ref, e_ref, u_refs[0])
    weights = (inv_ref, wx_ref, wy_ref, wz_ref)
    for k in range(passes):
        width = -(-(reach + passes - 1 - k) // per)
        level_pass(base - width, base + size + width, k, degree, lowest, zstep, *weights, e_ref, u_refs, packed, wb_ref)


def coarsen_rows(one, two, pair_ref, zstep):
    pair_ref[...] = one + two
    half = pair_ref.shape[0] // 2
    summed = pair_ref[pl.ds(0, half, 2), :] + pair_ref[pl.ds(1, half, 2), :]
    return (summed + ahead(summed, 1, zstep)) * 0.125


def pack_two(one, two):
    return jnp.where((lane_index(one.shape) & 1) == 0, one, behind(two, 1))


def coarsen_packed(value, pair_ref):
    pair_ref[...] = value
    half = pair_ref.shape[0] // 2
    summed = pair_ref[pl.ds(0, half, 2), :] + pair_ref[pl.ds(1, half, 2), :]
    summed = summed + ahead(summed, 1)
    return (summed + ahead(summed, 1, 2)) * 0.125


def spread_mask(lines, spread, ny):
    wide = jnp.dot(lines.astype(jnp.float32), spread, preferred_element_type=jnp.float32)
    tiles = [jnp.broadcast_to(wide[by : by + 1], (BRICK, wide.shape[1])) for by in range(ny // BRICK)]
    return jnp.concatenate(tiles, axis=0)


def spread_matrix(nbz, nz):
    shape = (nbz, nz)
    column, line = lax.broadcasted_iota(jnp.int32, shape, 1), lax.broadcasted_iota(jnp.int32, shape, 0)
    return jnp.where(column // BRICK == line, 1.0, 0.0)


def start_all(copies, sems):
    started = [pltpu.make_async_copy(src, dst, sems.at[n]) for n, (src, dst) in enumerate(copies)]
    for copy in started:
        copy.start()
    return started


def block_kernel(slots, src_hbm, kap_hbm, ab_hbm, brick_hbm, b_ref, a_ref, g_ref, to_even, to_odd, q_ref, *rest):
    y_outs, (bricks, pair_ref, sems) = rest[:slots], rest[slots:]
    nx, ny, nz = src_hbm.shape
    lower, upper = DEGREE, DEGREE + 1
    started = start_all([(brick_hbm, bricks), (kap_hbm, g_ref), (ab_hbm, a_ref), (src_hbm, b_ref)], sems)
    spread = spread_matrix(bricks.shape[2], nz)
    started[0].wait()
    started[1].wait()
    for bx in range(nx // BRICK):
        mask = spread_mask(bricks[bx], spread, ny)
        for x in range(bx * BRICK, (bx + 1) * BRICK):
            g_ref[x] = g_ref[x] * mask

    def packed_rows(field, ref):
        for j in range(nx // 4):
            cells = []
            for t in range(2):
                x = 4 * j + 2 * t
                scratch = pair_ref.at[(field * (nx // 4) + j) * 2 + t]
                cells.append(coarsen_rows(ref[x], ref[x + 1], scratch, 1))
            q_ref[field * (nx // 4) + j] = pack_two(*cells)

    packed_rows(0, g_ref)
    started[2].wait()
    packed_rows(1, a_ref)
    started[3].wait()

    even = lax.axis_index("dom") % 2 == 0
    for out, up in ((to_even, even), (to_odd, jnp.logical_not(even))):
        four = jnp.where(up, nx - lower, 0)
        five = jnp.where(up, nx - upper, 0)
        for j in range(lower):
            out[j] = b_ref[four + j]
            out[lower + j] = a_ref[four + j]
        for j in range(upper):
            out[2 * lower + j] = g_ref[five + j]

    for slot, out in enumerate(y_outs):
        at = pl.multiple_of(jnp.where(sends_up(slots, slot), ny - TILE, 0), TILE)
        for x in range(nx):
            out[0, x] = b_ref[x, pl.ds(at, TILE), :]
            out[1, x] = a_ref[x, pl.ds(at, TILE), :]
            out[2, x] = g_ref[x, pl.ds(at, TILE), :]


def sends_up(slots, slot):
    return lax.axis_index("grp") == 0 if slots == 1 else slot == 1


def slot_is_upper(slots, slot):
    return lax.axis_index("grp") == 0 if slots == 1 else slot == 0


def keep_near(value, is_upper, reach):
    rows = lax.broadcasted_iota(jnp.int32, value.shape, 0)
    size = value.shape[0]
    low = jnp.where(is_upper, 0, size - reach)
    high = jnp.where(is_upper, reach, size)
    return jnp.where((rows >= low) & (rows < high), value, 0.0)


def pack_rows(j, row, pair_ref):
    cells = []
    for t in range(2):
        x = 4 * j + 2 * t
        cells.append(coarsen_rows(row(x), row(x + 1), pair_ref.at[2 * j + t], 1))
    return pack_two(*cells)


def inner_packs(nx):
    first = -(-(DEGREE + 1) // 4)
    return range(first, nx // 4 - first)


class Joined:
    def __init__(self, own_ref, y_refs, field):
        self.own_ref, self.y_refs, self.field = own_ref, y_refs, field

    def __getitem__(self, x):
        parts = [self.own_ref[x]]
        for slot, y_ref in enumerate(self.y_refs):
            tile = y_ref[self.field, x]
            if self.field == 2:
                tile = keep_near(tile, slot_is_upper(len(self.y_refs), slot), DEGREE + 1)
            parts.append(tile)
        return jnp.concatenate(parts, axis=0)


class Rim:
    def __init__(self, nx, new_ref, before=None):
        self.nx, self.new_ref, self.before, self.written = nx, new_ref, before, set()

    def place(self, x):
        rows = self.new_ref.shape[0]
        return x + DEGREE + 1 if x < self.nx // 2 else rows - (self.nx + DEGREE + 1) + x

    def __getitem__(self, x):
        return self.new_ref[self.place(x)] if x in self.written else self.before[x]

    def __setitem__(self, x, value):
        self.new_ref[self.place(x)] = value
        self.written.add(x)


def inner_kernel(slots, *refs):
    b_in, a_in, g_in = refs[:3]
    y_refs = refs[3 : 3 + slots]
    wx, wy, wz, inv, d_ref, e_ref, u0, u1, u2, u3, it_out, res_out, s_ref, pair_ref = refs[3 + slots :]
    nx, ny, _ = b_in.shape
    b_ref, a_ref, g_ref = (Joined(ref, y_refs, field) for field, ref in enumerate((b_in, a_in, g_in)))
    u_refs = (u0, u1, u2, u3)
    level_setup(1, nx - 1, 1, STEP_SCALE, g_ref, a_ref, wx, wy, wz, inv, d_ref)
    level_start(1, nx - 1, SMOOTH_LOW, b_ref, inv, e_ref, u0)
    for k in range(DEGREE):
        level_pass(2 + k, nx - 2 - k, k, DEGREE, SMOOTH_LOW, 1, inv, wx, wy, wz, e_ref, u_refs)

    def finish(x):
        it_out[x] = (u0[x, :ny] + u1[x, :ny]) + (u2[x, :ny] + u3[x, :ny])
        res_out[x] = d_ref[x, :ny] * e_ref[x, :ny]

    rows_loop(DEGREE + 1, nx - DEGREE - 1, finish)
    for j in inner_packs(nx):
        s_ref[j] = pack_rows(j, lambda x: res_out[x], pair_ref)


def corner_kernel(slots, ra_ref, rb_ref, _, *outs):
    rows, ny, _ = ra_ref.shape
    for slot, out in enumerate(outs):
        at = pl.multiple_of(jnp.where(sends_up(slots, slot), ny - TILE, 0), TILE)
        for j in range(rows):
            out[0, j] = ra_ref[j, pl.ds(at, TILE), :]
            out[1, j] = rb_ref[j, pl.ds(at, TILE), :]


def stack_kernel(count, *refs):
    out = refs[-1]
    spare = refs[0].shape[0] - out.shape[1]
    first = jnp.where(lax.axis_index("grp") == 0, spare, 0) if spare else 0
    for part in range(count):
        for j in range(out.shape[1]):
            out[part, j] = refs[part][first + j]


def stack(arrays, *earlier, spare=0):
    rows, *rest = arrays[0].shape
    shape = (len(arrays), rows - spare, *rest)
    (out,) = call(functools.partial(stack_kernel, len(arrays)), (*arrays, *earlier), [shape])
    return out


def rim_kernel(slots, *refs):
    b_in, a_in, g_in = refs[:3]
    y_refs = refs[3 : 3 + slots]
    before, refs = refs[3 + slots : 13 + slots], refs[13 + slots :]
    res_in, s_in, ra_ref, rb_ref = refs[:4]
    c_refs = refs[4 : 4 + slots]
    it_out, res_out, s_ref = refs[4 + slots : 7 + slots]
    scratch, pair_ref = refs[7 + slots : -1], refs[-1]
    nx, ny, _ = b_in.shape
    lower, upper = DEGREE, DEGREE + 1

    b_ref, a_ref, g_ref = (
        Rim(nx, scratch[field], Joined(ref, y_refs, field)) for field, ref in enumerate((b_in, a_in, g_in))
    )
    wx, wy, wz, inv, d_ref, e_ref, *u_refs = (Rim(nx, new, old) for new, old in zip(scratch[3:], before))

    even = lax.axis_index("dom") % 2 == 0

    def received(j, is_above):
        from_even = even if is_above else jnp.logical_not(even)
        parts = [jnp.where(from_even, ra_ref[j], rb_ref[j])]
        for slot in range(slots):
            is_upper = slot_is_upper(slots, slot)
            tile = jnp.where(from_even, c_refs[slot][0, j], c_refs[slot][1, j])
            if j >= 2 * lower:
                tile = keep_near(tile, is_upper, upper)
            parts.append(tile)
        return jnp.concatenate(parts, axis=0)

    for is_above in (False, True):
        for j in range(lower):
            x = nx + j if is_above else j - lower
            b_ref[x] = received(j, is_above)
            a_ref[x] = received(lower + j, is_above)
        for j in range(upper):
            x = nx + j if is_above else j - upper
            g_ref[x] = received(2 * lower + j, is_above)

    for lo, hi in ((-lower, 1), (nx - 1, nx + lower)):
        level_setup(lo, hi, 1, STEP_SCALE, g_ref, a_ref, wx, wy, wz, inv, d_ref)
        level_start(lo, hi, SMOOTH_LOW, b_ref, inv, e_ref, u_refs[0])
    for k in range(DEGREE):
        out = DEGREE - 1 - k
        for lo, hi in ((-out, 2 + k), (nx - 2 - k, nx + out)):
            level_pass(lo, hi, k, DEGREE, SMOOTH_LOW, 1, inv, wx, wy, wz, e_ref, u_refs)

    place = {x: x for x in range(upper)}
    place.update({nx - upper + x: upper + x for x in range(upper)})
    for x, at in place.items():
        total = [u_ref[x][:ny] for u_ref in u_refs]
        it_out[at] = (total[0] + total[1]) + (total[2] + total[3])
        res_out[at] = d_ref[x][:ny] * e_ref[x][:ny]
    inner = inner_packs(nx)
    for j in range(nx // 4):
        if j in inner:
            s_ref[j] = s_in[j]
        else:
            s_ref[j] = pack_rows(j, lambda x: res_out[place[x]] if x in place else res_in[x], pair_ref)


def output_kernel(it_in, res_in, it_rim, res_rim, it_out, res_out, done_ref, sems):
    done_ref[...] = jnp.zeros_like(done_ref)
    nx = it_in.shape[0]
    rim = DEGREE + 1
    copies = []
    for inside, near, out in ((it_in, it_rim, it_out), (res_in, res_rim, res_out)):
        middle = pl.ds(rim, nx - 2 * rim)
        copies += [
            (inside.at[middle], out.at[middle]),
            (near.at[pl.ds(0, rim)], out.at[pl.ds(0, rim)]),
            (near.at[pl.ds(rim, rim)], out.at[pl.ds(nx - rim, rim)]),
        ]
    for copy in start_all(copies, sems):
        copy.wait()


def compact(value, step, first=0):
    nz = value.shape[-1]
    shape = (nz, nz // step)
    pick = jnp.where(
        lax.broadcasted_iota(jnp.int32, shape, 0) == first + step * lax.broadcasted_iota(jnp.int32, shape, 1), 1.0, 0.0
    )
    return jnp.dot(value, pick, preferred_element_type=jnp.float32, precision=lax.Precision.HIGHEST)


def placed_parts(slots, rows, own_refs, around_refs, unread=0):
    parts = [(rows, slot, ref) for slot, ref in enumerate(own_refs)]
    if slots == 1:
        core = lax.axis_index("grp")
        for which, (ref, above) in enumerate(zip(around_refs, (core == 0, core == 1))):
            start = jnp.where(above, 2 * rows, unread)
            parts += [(start, 0, ref.at[1 - which]), (start, 1, ref.at[which])]
    else:
        even = lax.axis_index("dom") % 2 == 0
        for which, above in enumerate((even, jnp.logical_not(even))):
            start = jnp.where(above, 2 * rows, 0)
            parts += [(start, slot, ref.at[which]) for slot, ref in enumerate(around_refs)]
    return parts


def coefficient_kernel(slots, *refs):
    own_refs, around_refs, refs = refs[: 1 + slots], refs[1 + slots : 2 + 2 * slots], refs[2 + 2 * slots :]
    wx, wy, wz, wb, inv, d_ref, cwx, cwy, cwz, cinv, a_ref, g_ref, ca, cg, cd, pair_ref = refs
    rows, ny = own_refs[0].shape[0] // 2, own_refs[0].shape[1]
    for start, slot, q_ref in placed_parts(slots, rows, own_refs, around_refs):
        at = slice(slot * ny, (slot + 1) * ny)
        for j in range(rows):
            g_row = q_ref[j]
            if slot:
                g_row = keep_near(g_row, slot_is_upper(slots, slot - 1), ny - 1)
            g_ref[start + j, at] = g_row
            a_ref[start + j, at] = q_ref[rows + j]

    width = -(-(2 * (COARSE_DEGREE - 1) + DEGREE) // 2)
    level_setup(rows - width, 2 * rows + width, 2, STEP_SCALE / 4.0, g_ref, a_ref, wx, wy, wz, inv, d_ref, True, wb)

    coarse_rows = cg.shape[0]
    def coefficients(i):
        row = rows - COARSE_DEGREE + i
        g = g_ref[row]
        whole = coarsen_packed(positive(g), pair_ref.at[3 * i]) > 0.75
        first = (lane_index(whole.shape) & 3) == 0
        cg[i] = jnp.where(whole & first, coarsen_packed(g, pair_ref.at[3 * i + 1]), 0.0)
        ca[i] = coarsen_packed(a_ref[row], pair_ref.at[3 * i + 2])

    rows_loop(0, coarse_rows, coefficients, block=10)
    level_setup(1, coarse_rows - 1, 4, STEP_SCALE / 16.0, cg, ca, cwx, cwy, cwz, cinv, cd)


def coarse_kernel(slots, *refs):
    own_refs, around_refs, refs = refs[: 1 + slots], refs[1 + slots : 2 + 2 * slots], refs[2 + 2 * slots :]
    wx, wy, wz, wb, inv, d_ref, cwx, cwy, cwz, cinv, mid_out, coarse_out = refs[:12]
    b_ref, e_ref, u0, u1, u2, u3, cb, ce, v0, v1, v2, v3, v4, v5, pair_ref = refs[12:]
    rows, ny, nz = own_refs[0].shape
    unread = rows - around_refs[0].shape[1]
    for start, slot, s_ref in placed_parts(slots, rows, own_refs, around_refs, unread):
        at = slice(slot * ny, (slot + 1) * ny)
        for j in range(s_ref.shape[0]):
            b_ref[start + j, at] = s_ref[j]

    reach = 2 * (COARSE_DEGREE - 1)
    u_refs = (u0, u1, u2, u3)
    updates = [Circular(u_ref) for u_ref in u_refs]
    level_sweeps(rows, rows, reach, DEGREE, SMOOTH_LOW, True, 2, b_ref, inv, wx, wy, wz, e_ref, updates, True, wb)

    total = u0[rows : 2 * rows, TILE : TILE + ny]
    for u_ref in u_refs[1:]:
        total = total + u_ref[rows : 2 * rows, TILE : TILE + ny]
    total = total.reshape(rows * ny, nz)
    for t in range(2):
        lines = compact(total, 2, t).reshape(rows, ny, nz // 2)
        for j in range(rows):
            mid_out[2 * j + t] = lines[j]

    half, cny = rows, ny // 2
    cbase = COARSE_DEGREE
    def source(i):
        row = rows - cbase + i
        cb[i] = coarsen_packed(d_ref[row] * e_ref[row], pair_ref.at[i])

    rows_loop(1, half + 2 * cbase - 1, source)
    v_refs = (v0, v1, v2, v3, v4, v5)
    level_sweeps(cbase, half, 0, COARSE_DEGREE, COARSE_LOW, False, 4, cb, cinv, cwx, cwy, cwz, ce, v_refs)
    total = v0[cbase : cbase + half, :cny]
    for v_ref in v_refs[1:]:
        total = total + v_ref[cbase : cbase + half, :cny]
    coarse_out[...] = compact(total.reshape(half * cny, nz), 4).reshape(half, cny, nz // 4)


def call(kernel, ins, outs, scratch=(), in_hbm=0, out_hbm=0):
    vmem, hbm = pl.BlockSpec(memory_space=pltpu.VMEM), pl.BlockSpec(memory_space=pltpu.HBM)
    return pl.pallas_call(
        kernel,
        out_shape=[jax.ShapeDtypeStruct(shape, jnp.float32) for shape in outs],
        in_specs=[hbm] * in_hbm + [vmem] * (len(ins) - in_hbm),
        out_specs=[hbm] * out_hbm + [vmem] * (len(outs) - out_hbm),
        scratch_shapes=[pltpu.VMEM(shape, jnp.float32) if isinstance(shape, tuple) else shape for shape in scratch],
        compiler_params=pltpu.CompilerParams(vmem_limit_bytes=VMEM_BYTES),
    )(*ins)


def body(source, conductivity, absorption, brick_mask):
    doms, grps = lax.axis_size("dom"), lax.axis_size("grp")
    slots = min(grps - 1, 2)
    nx, ny, nz = source.shape
    lower, upper = DEGREE, DEGREE + 1

    def pairing(first):
        pairs = [(i, i + 1) for i in range(first, doms - 1, 2)]
        return pairs + [(j, i) for i, j in pairs]

    def swap_even(array):
        return lax.ppermute(array, "dom", pairing(0))

    def swap_odd(array):
        return lax.ppermute(array, "dom", pairing(1))

    downward = [(i + 1, i) for i in range(grps - 1)]
    upward = [(i, i + 1) for i in range(grps - 1)]

    def along_grp(arrays):
        if slots == 0:
            return []
        if slots == 1:
            return [lax.ppermute(arrays[0], "grp", downward + upward)]
        return [lax.ppermute(arrays[0], "grp", downward), lax.ppermute(arrays[-1], "grp", upward)]

    crossing = []
    for i in range(doms - 1):
        crossing += [(i * grps, (i + 1) * grps + 1), ((i + 1) * grps + 1, i * grps)]

    def send_around(own, beside, spare=0):
        if slots == 1:
            both = stack([own, beside[0]], spare=spare)
            return [lax.ppermute(both, ("dom", "grp"), crossing)], both
        return [swap_even(own), swap_odd(own)], own

    def share_around(arrays, *earlier):
        both = stack(arrays, *earlier)
        both = both.reshape(2, *both.shape[-3:])
        return [both, *along_grp([both])]

    fields = [pltpu.with_memory_space_constraint(x, pltpu.HBM) for x in (source, conductivity, absorption, brick_mask)]
    bricks = pltpu.VMEM(brick_mask.shape, brick_mask.dtype)
    payload = (2 * lower + upper, ny, nz)
    packed = nx // 4
    small = (packed, ny // 2, nz)
    b_own, a_own, g_own, to_even, to_odd, coeffs, *edges = call(
        functools.partial(block_kernel, slots),
        fields,
        [source.shape] * 3 + [payload] * 2 + [(2 * packed, ny // 2, nz)] + [(3, nx, TILE, nz)] * slots,
        [bricks, (4 * packed, ny, nz), pltpu.SemaphoreType.DMA((4,))],
        in_hbm=4,
    )
    from_even, from_odd = swap_even(to_even), swap_odd(to_odd)
    own = (b_own, a_own, g_own, *along_grp(edges))
    coeffs_beside = along_grp([coeffs])
    coeffs_sent, _ = send_around(coeffs, coeffs_beside)

    wide = (nx, ny + slots * TILE, nz)
    pairs = (nx // 2, ny, nz)
    *state, it_inner, res_inner, s_inner = call(
        functools.partial(inner_kernel, slots),
        own,
        [wide] * 10 + [source.shape, source.shape, small],
        [pairs],
    )
    corners = call(
        functools.partial(corner_kernel, slots),
        (from_even, from_odd, s_inner),
        [(2, payload[0], TILE, nz)] * slots,
    )
    corners_beside = along_grp(corners)
    rim = (2 * upper, ny, nz)
    near = (4 * upper + 2, ny + slots * TILE, nz)
    it_rim, res_rim, mid_source = call(
        functools.partial(rim_kernel, slots),
        (*own, *state, res_inner, s_inner, from_even, from_odd, *corners_beside),
        [rim, rim, small],
        [near] * 13 + [pairs],
    )
    fine_iterate, fine_residual, written = call(
        output_kernel,
        (it_inner, res_inner, it_rim, res_rim),
        [source.shape, source.shape, (TILE, nz)],
        [pltpu.SemaphoreType.DMA((6,))],
        out_hbm=2,
    )

    source_beside = along_grp([mid_source])
    unread = packed - -(-(2 * (COARSE_DEGREE - 1) + DEGREE) // 2)
    source_sent, sending = send_around(mid_source, source_beside, unread)
    q_ins = [coeffs, *coeffs_beside, *share_around(coeffs_sent, sending)]
    mid_y = (1 + slots) * ny // 2
    mid_wide = (3 * packed, mid_y, nz)
    coarse_rows = nx // 4 + 2 * COARSE_DEGREE
    coarse_wide = (coarse_rows, mid_y // 2, nz)
    weights = call(
        functools.partial(coefficient_kernel, slots),
        q_ins,
        [mid_wide] * 6 + [coarse_wide] * 4,
        [mid_wide] * 2 + [coarse_wide] * 3 + [(3 * coarse_rows, mid_y, nz)],
    )
    s_ins = [mid_source, *source_beside, *share_around(source_sent, weights[-1], written)]
    mid_iterate, coarse_iterate = call(
        functools.partial(coarse_kernel, slots),
        (*s_ins, *weights),
        [(nx // 2, ny // 2, nz // 2), (nx // 4, ny // 4, nz // 4)],
        [mid_wide] * 2 + [(3 * packed, mid_y + 2 * TILE, nz)] * 4 + [coarse_wide] * 8 + [(coarse_rows, mid_y, nz)],
    )
    return (fine_iterate, fine_residual, mid_iterate, coarse_iterate)


def solution(mesh):
    spec = P("dom", "grp", None)
    return jax.shard_map(body, mesh=mesh, in_specs=(spec,) * 4, out_specs=(spec,) * 4, check_vma=False)
```

```python
import functools

import jax
import jax.numpy as jnp
from jax import lax
from jax.experimental import pallas as pl
from jax.experimental.pallas import tpu as pltpu
from jax.sharding import PartitionSpec as P

DEGREE = 4
COARSE_DEGREE = 6

STEP_SCALE = 4.0
SMOOTH_LOW = 0.3
SMOOTH_HIGH = 2.0
COARSE_LOW = 0.05

BRICK = 8
TILE = 8
VMEM_BYTES = 24 * 1024 * 1024


def chebyshev_constants(degree, lowest, highest):
    middle = (highest + lowest) / 2.0
    spread = (highest - lowest) / 2.0
    relative = middle / spread
    previous = 1.0 / relative
    steps = []
    for _ in range(degree - 1):
        following = 1.0 / (2.0 * relative - previous)
        steps.append((following * previous, 2.0 * following / spread))
        previous = following
    return 1.0 / middle, steps


def lane_index(shape):
    return lax.broadcasted_iota(jnp.int32, shape, len(shape) - 1)


def ahead(value, axis, step=1):
    return pltpu.roll(value, value.shape[axis] - step, axis)


def behind(value, axis, step=1):
    return pltpu.roll(value, step, axis)


def positive(value):
    return jnp.where(value > 0.0, 1.0, 0.0)


def rows_loop(start, stop, body, block=50):
    count = stop - start
    if count <= 0:
        return
    loops = -(-count // block)
    size = count // loops

    def run(j, carry):
        for t in range(size):
            body(start + j * size + t)
        return carry

    if loops > 1:
        lax.fori_loop(0, loops, run, 0)
    else:
        run(0, 0)
    for i in range(start + loops * size, stop):
        body(i)


def next_row(value, following, packed):
    if not packed:
        return following
    return jnp.where((lane_index(value.shape) & 1) == 0, ahead(value, 1), behind(following, 1))


def previous_row(before, value, packed):
    if not packed:
        return before
    return jnp.where((lane_index(value.shape) & 1) == 0, ahead(before, 1), behind(value, 1))


def level_setup(lo, hi, zstep, factor, g_ref, a_ref, wx_ref, wy_ref, wz_ref, inv_ref, d_ref, packed=False, wb_ref=None):
    half = 0.5 * factor

    def weight_x(i):
        here = g_ref[i]
        there = next_row(here, g_ref[i + 1], packed)
        wx_ref[i] = jnp.where((here > 0.0) & (there > 0.0), half * (here + there), 0.0)

    weight_x(lo - 1)

    def row(i):
        weight_x(i)
        here = g_ref[i]
        lanes = lane_index(here.shape)
        inside = here > 0.0
        there_y = ahead(here, 0)
        there_z = ahead(here, 1, zstep)
        wy = jnp.where(inside & (there_y > 0.0), half * (here + there_y), 0.0)
        wz = jnp.where(inside & (there_z > 0.0) & (lanes < here.shape[1] - zstep), half * (here + there_z), 0.0)
        wy_ref[i] = wy
        wz_ref[i] = wz
        wx = wx_ref[i]
        wb = behind(wy, 0)
        if wb_ref is not None:
            wb_ref[i] = wb
        faces = [wx, previous_row(wx_ref[i - 1], wx, packed), wy, wb, wz, behind(wz, 1, zstep)]
        wall = factor * a_ref[i]
        diagonal = 1.0 + jnp.where(faces[0] > 0.0, faces[0], wall)
        for face in faces[1:]:
            diagonal = diagonal + jnp.where(face > 0.0, face, wall)
        d_ref[i] = diagonal
        inv_ref[i] = jnp.where(inside, 1.0 / diagonal, 0.0)

    rows_loop(lo, hi, row, block=15)


class Circular:
    def __init__(self, ref):
        self.ref, self.size = ref, ref.shape[1] - 2 * TILE

    def __getitem__(self, i):
        return self.ref[i, TILE : TILE + self.size]

    def __setitem__(self, i, value):
        self.ref[i, TILE : TILE + self.size] = value
        self.ref[i, :TILE] = value[self.size - TILE :]
        self.ref[i, TILE + self.size :] = value[:TILE]

    def shifted(self, i, step):
        return self.ref[i, TILE + step : TILE + step + self.size]


def level_start(lo, hi, lowest, b_ref, inv_ref, e_ref, u_ref):
    first, _ = chebyshev_constants(1, lowest, SMOOTH_HIGH)

    def row(i):
        e = inv_ref[i] * b_ref[i]
        e_ref[i] = e
        u_ref[i] = e * first

    rows_loop(lo, hi, row)


def level_pass(lo, hi, k, degree, lowest, zstep, inv_ref, wx_ref, wy_ref, wz_ref, e_ref, u_refs, packed=False, wb_ref=None):
    _, steps = chebyshev_constants(degree, lowest, SMOOTH_HIGH)
    old = u_refs[k]
    kept = {}

    def row(i):
        if isinstance(i, int) and i - 1 in kept:
            u, before = kept.pop(i - 1)
        else:
            u, before = old[i], wx_ref[i - 1] * old[i - 1]
        following = old[i + 1]
        wx = wx_ref[i]
        wy = wy_ref[i]
        wz = wz_ref[i]
        weighted = wx * u
        if isinstance(i, int):
            kept[i] = following, weighted
        coupled = wx * next_row(u, following, packed) + previous_row(before, weighted, packed)
        if wb_ref is None:
            coupled = coupled + (wy * ahead(u, 0) + behind(wy * u, 0))
        else:
            coupled = coupled + (wy * old.shifted(i, 1) + wb_ref[i] * old.shifted(i, -1))
        coupled = coupled + (wz * ahead(u, 1, zstep) + behind(wz * u, 1, zstep))
        e = e_ref[i] - u + inv_ref[i] * coupled
        e_ref[i] = e
        if k + 1 < degree:
            u_refs[k + 1][i] = steps[k][0] * u + steps[k][1] * e

    rows_loop(lo, hi, row)


def level_sweeps(
    base, size, reach, degree, lowest, keep, zstep, b_ref, inv_ref, wx_ref, wy_ref, wz_ref, e_ref, u_refs, packed=False, wb_ref=None
):
    passes = degree if keep else degree - 1
    per = 2 if packed else 1
    width = -(-(reach + passes) // per)
    level_start(base - width, base + size + width, lowest, b_ref, inv_ref, e_ref, u_refs[0])
    weights = (inv_ref, wx_ref, wy_ref, wz_ref)
    for k in range(passes):
        width = -(-(reach + passes - 1 - k) // per)
        level_pass(base - width, base + size + width, k, degree, lowest, zstep, *weights, e_ref, u_refs, packed, wb_ref)


def coarsen_rows(one, two, pair_ref, zstep):
    pair_ref[...] = one + two
    half = pair_ref.shape[0] // 2
    summed = pair_ref[pl.ds(0, half, 2), :] + pair_ref[pl.ds(1, half, 2), :]
    return (summed + ahead(summed, 1, zstep)) * 0.125


def pack_two(one, two):
    return jnp.where((lane_index(one.shape) & 1) == 0, one, behind(two, 1))


def coarsen_packed(value, pair_ref):
    pair_ref[...] = value
    half = pair_ref.shape[0] // 2
    summed = pair_ref[pl.ds(0, half, 2), :] + pair_ref[pl.ds(1, half, 2), :]
    summed = summed + ahead(summed, 1)
    return (summed + ahead(summed, 1, 2)) * 0.125


def spread_mask(lines, spread, ny):
    wide = jnp.dot(lines.astype(jnp.float32), spread, preferred_element_type=jnp.float32)
    tiles = [jnp.broadcast_to(wide[by : by + 1], (BRICK, wide.shape[1])) for by in range(ny // BRICK)]
    return jnp.concatenate(tiles, axis=0)


def spread_matrix(nbz, nz):
    shape = (nbz, nz)
    column, line = lax.broadcasted_iota(jnp.int32, shape, 1), lax.broadcasted_iota(jnp.int32, shape, 0)
    return jnp.where(column // BRICK == line, 1.0, 0.0)


def start_all(copies, sems):
    started = [pltpu.make_async_copy(src, dst, sems.at[n]) for n, (src, dst) in enumerate(copies)]
    for copy in started:
        copy.start()
    return started


def block_kernel(slots, src_hbm, kap_hbm, ab_hbm, brick_hbm, b_ref, a_ref, g_ref, to_even, to_odd, q_ref, *rest):
    y_outs, (bricks, pair_ref, sems) = rest[:slots], rest[slots:]
    nx, ny, nz = src_hbm.shape
    lower, upper = DEGREE, DEGREE + 1
    started = start_all([(brick_hbm, bricks), (kap_hbm, g_ref), (ab_hbm, a_ref), (src_hbm, b_ref)], sems)
    spread = spread_matrix(bricks.shape[2], nz)
    started[0].wait()
    started[1].wait()
    for bx in range(nx // BRICK):
        mask = spread_mask(bricks[bx], spread, ny)
        for x in range(bx * BRICK, (bx + 1) * BRICK):
            g_ref[x] = g_ref[x] * mask

    def packed_rows(field, ref):
        for j in range(nx // 4):
            cells = []
            for t in range(2):
                x = 4 * j + 2 * t
                scratch = pair_ref.at[(field * (nx // 4) + j) * 2 + t]
                cells.append(coarsen_rows(ref[x], ref[x + 1], scratch, 1))
            q_ref[field * (nx // 4) + j] = pack_two(*cells)

    packed_rows(0, g_ref)
    started[2].wait()
    packed_rows(1, a_ref)
    started[3].wait()

    even = lax.axis_index("dom") % 2 == 0
    for out, up in ((to_even, even), (to_odd, jnp.logical_not(even))):
        four = jnp.where(up, nx - lower, 0)
        five = jnp.where(up, nx - upper, 0)
        for j in range(lower):
            out[j] = b_ref[four + j]
            out[lower + j] = a_ref[four + j]
        for j in range(upper):
            out[2 * lower + j] = g_ref[five + j]

    for slot, out in enumerate(y_outs):
        at = pl.multiple_of(jnp.where(sends_up(slots, slot), ny - TILE, 0), TILE)
        for x in range(nx):
            out[0, x] = b_ref[x, pl.ds(at, TILE), :]
            out[1, x] = a_ref[x, pl.ds(at, TILE), :]
            out[2, x] = g_ref[x, pl.ds(at, TILE), :]


def sends_up(slots, slot):
    return lax.axis_index("grp") == 0 if slots == 1 else slot == 1


def slot_is_upper(slots, slot):
    return lax.axis_index("grp") == 0 if slots == 1 else slot == 0


def keep_near(value, is_upper, reach):
    rows = lax.broadcasted_iota(jnp.int32, value.shape, 0)
    size = value.shape[0]
    low = jnp.where(is_upper, 0, size - reach)
    high = jnp.where(is_upper, reach, size)
    return jnp.where((rows >= low) & (rows < high), value, 0.0)


def pack_rows(j, row, pair_ref):
    cells = []
    for t in range(2):
        x = 4 * j + 2 * t
        cells.append(coarsen_rows(row(x), row(x + 1), pair_ref.at[2 * j + t], 1))
    return pack_two(*cells)


def inner_packs(nx):
    first = -(-(DEGREE + 1) // 4)
    return range(first, nx // 4 - first)


class Joined:
    def __init__(self, own_ref, y_refs, field):
        self.own_ref, self.y_refs, self.field = own_ref, y_refs, field

    def __getitem__(self, x):
        parts = [self.own_ref[x]]
        for slot, y_ref in enumerate(self.y_refs):
            tile = y_ref[self.field, x]
            if self.field == 2:
                tile = keep_near(tile, slot_is_upper(len(self.y_refs), slot), DEGREE + 1)
            parts.append(tile)
        return jnp.concatenate(parts, axis=0)


class Rim:
    def __init__(self, nx, new_ref, before=None):
        self.nx, self.new_ref, self.before, self.written = nx, new_ref, before, set()

    def place(self, x):
        rows = self.new_ref.shape[0]
        return x + DEGREE + 1 if x < self.nx // 2 else rows - (self.nx + DEGREE + 1) + x

    def __getitem__(self, x):
        return self.new_ref[self.place(x)] if x in self.written else self.before[x]

    def __setitem__(self, x, value):
        self.new_ref[self.place(x)] = value
        self.written.add(x)


def inner_kernel(slots, *refs):
    b_in, a_in, g_in = refs[:3]
    y_refs = refs[3 : 3 + slots]
    wx, wy, wz, inv, d_ref, e_ref, u0, u1, u2, u3, it_out, res_out, s_ref, pair_ref = refs[3 + slots :]
    nx, ny, _ = b_in.shape
    b_ref, a_ref, g_ref = (Joined(ref, y_refs, field) for field, ref in enumerate((b_in, a_in, g_in)))
    u_refs = (u0, u1, u2, u3)
    level_setup(1, nx - 1, 1, STEP_SCALE, g_ref, a_ref, wx, wy, wz, inv, d_ref)
    level_start(1, nx - 1, SMOOTH_LOW, b_ref, inv, e_ref, u0)
    for k in range(DEGREE):
        level_pass(2 + k, nx - 2 - k, k, DEGREE, SMOOTH_LOW, 1, inv, wx, wy, wz, e_ref, u_refs)

    def finish(x):
        it_out[x] = (u0[x, :ny] + u1[x, :ny]) + (u2[x, :ny] + u3[x, :ny])
        res_out[x] = d_ref[x, :ny] * e_ref[x, :ny]

    rows_loop(DEGREE + 1, nx - DEGREE - 1, finish)
    for j in inner_packs(nx):
        s_ref[j] = pack_rows(j, lambda x: res_out[x], pair_ref)


def corner_kernel(slots, ra_ref, rb_ref, _, *outs):
    rows, ny, _ = ra_ref.shape
    for slot, out in enumerate(outs):
        at = pl.multiple_of(jnp.where(sends_up(slots, slot), ny - TILE, 0), TILE)
        for j in range(rows):
            out[0, j] = ra_ref[j, pl.ds(at, TILE), :]
            out[1, j] = rb_ref[j, pl.ds(at, TILE), :]


def stack_kernel(count, *refs):
    out = refs[-1]
    spare = refs[0].shape[0] - out.shape[1]
    first = jnp.where(lax.axis_index("grp") == 0, spare, 0) if spare else 0
    for part in range(count):
        for j in range(out.shape[1]):
            out[part, j] = refs[part][first + j]


def stack(arrays, *earlier, spare=0):
    rows, *rest = arrays[0].shape
    shape = (len(arrays), rows - spare, *rest)
    (out,) = call(functools.partial(stack_kernel, len(arrays)), (*arrays, *earlier), [shape])
    return out


def rim_kernel(slots, *refs):
    b_in, a_in, g_in = refs[:3]
    y_refs = refs[3 : 3 + slots]
    before, refs = refs[3 + slots : 13 + slots], refs[13 + slots :]
    res_in, s_in, ra_ref, rb_ref = refs[:4]
    c_refs = refs[4 : 4 + slots]
    it_out, res_out, s_ref = refs[4 + slots : 7 + slots]
    scratch, pair_ref = refs[7 + slots : -1], refs[-1]
    nx, ny, _ = b_in.shape
    lower, upper = DEGREE, DEGREE + 1

    b_ref, a_ref, g_ref = (
        Rim(nx, scratch[field], Joined(ref, y_refs, field)) for field, ref in enumerate((b_in, a_in, g_in))
    )
    wx, wy, wz, inv, d_ref, e_ref, *u_refs = (Rim(nx, new, old) for new, old in zip(scratch[3:], before))

    even = lax.axis_index("dom") % 2 == 0

    def received(j, is_above):
        from_even = even if is_above else jnp.logical_not(even)
        parts = [jnp.where(from_even, ra_ref[j], rb_ref[j])]
        for slot in range(slots):
            is_upper = slot_is_upper(slots, slot)
            tile = jnp.where(from_even, c_refs[slot][0, j], c_refs[slot][1, j])
            if j >= 2 * lower:
                tile = keep_near(tile, is_upper, upper)
            parts.append(tile)
        return jnp.concatenate(parts, axis=0)

    for is_above in (False, True):
        for j in range(lower):
            x = nx + j if is_above else j - lower
            b_ref[x] = received(j, is_above)
            a_ref[x] = received(lower + j, is_above)
        for j in range(upper):
            x = nx + j if is_above else j - upper
            g_ref[x] = received(2 * lower + j, is_above)

    for lo, hi in ((-lower, 1), (nx - 1, nx + lower)):
        level_setup(lo, hi, 1, STEP_SCALE, g_ref, a_ref, wx, wy, wz, inv, d_ref)
        level_start(lo, hi, SMOOTH_LOW, b_ref, inv, e_ref, u_refs[0])
    for k in range(DEGREE):
        out = DEGREE - 1 - k
        for lo, hi in ((-out, 2 + k), (nx - 2 - k, nx + out)):
            level_pass(lo, hi, k, DEGREE, SMOOTH_LOW, 1, inv, wx, wy, wz, e_ref, u_refs)

    place = {x: x for x in range(upper)}
    place.update({nx - upper + x: upper + x for x in range(upper)})
    for x, at in place.items():
        total = [u_ref[x][:ny] for u_ref in u_refs]
        it_out[at] = (total[0] + total[1]) + (total[2] + total[3])
        res_out[at] = d_ref[x][:ny] * e_ref[x][:ny]
    inner = inner_packs(nx)
    for j in range(nx // 4):
        if j in inner:
            s_ref[j] = s_in[j]
        else:
            s_ref[j] = pack_rows(j, lambda x: res_out[place[x]] if x in place else res_in[x], pair_ref)


def output_kernel(it_in, res_in, it_rim, res_rim, it_out, res_out, done_ref, sems):
    done_ref[...] = jnp.zeros_like(done_ref)
    nx = it_in.shape[0]
    rim = DEGREE + 1
    copies = []
    for inside, near, out in ((it_in, it_rim, it_out), (res_in, res_rim, res_out)):
        middle = pl.ds(rim, nx - 2 * rim)
        copies += [
            (inside.at[middle], out.at[middle]),
            (near.at[pl.ds(0, rim)], out.at[pl.ds(0, rim)]),
            (near.at[pl.ds(rim, rim)], out.at[pl.ds(nx - rim, rim)]),
        ]
    for copy in start_all(copies, sems):
        copy.wait()


def compact(value, step, first=0):
    nz = value.shape[-1]
    shape = (nz, nz // step)
    pick = jnp.where(
        lax.broadcasted_iota(jnp.int32, shape, 0) == first + step * lax.broadcasted_iota(jnp.int32, shape, 1), 1.0, 0.0
    )
    return jnp.dot(value, pick, preferred_element_type=jnp.float32, precision=lax.Precision.HIGHEST)


def placed_parts(slots, rows, own_refs, around_refs, unread=0):
    parts = [(rows, slot, ref) for slot, ref in enumerate(own_refs)]
    if slots == 1:
        core = lax.axis_index("grp")
        for which, (ref, above) in enumerate(zip(around_refs, (core == 0, core == 1))):
            start = jnp.where(above, 2 * rows, unread)
            parts += [(start, 0, ref.at[1 - which]), (start, 1, ref.at[which])]
    else:
        even = lax.axis_index("dom") % 2 == 0
        for which, above in enumerate((even, jnp.logical_not(even))):
            start = jnp.where(above, 2 * rows, 0)
            parts += [(start, slot, ref.at[which]) for slot, ref in enumerate(around_refs)]
    return parts


def coefficient_kernel(slots, *refs):
    own_refs, around_refs, refs = refs[: 1 + slots], refs[1 + slots : 2 + 2 * slots], refs[2 + 2 * slots :]
    wx, wy, wz, wb, inv, d_ref, cwx, cwy, cwz, cwb, cinv, a_ref, g_ref, ca, cg, cd, pair_ref = refs
    rows, ny = own_refs[0].shape[0] // 2, own_refs[0].shape[1]
    for start, slot, q_ref in placed_parts(slots, rows, own_refs, around_refs):
        at = slice(slot * ny, (slot + 1) * ny)
        for j in range(rows):
            g_row = q_ref[j]
            if slot:
                g_row = keep_near(g_row, slot_is_upper(slots, slot - 1), ny - 1)
            g_ref[start + j, at] = g_row
            a_ref[start + j, at] = q_ref[rows + j]

    width = -(-(2 * (COARSE_DEGREE - 1) + DEGREE) // 2)
    level_setup(rows - width, 2 * rows + width, 2, STEP_SCALE / 4.0, g_ref, a_ref, wx, wy, wz, inv, d_ref, True, wb)

    coarse_rows = cg.shape[0]
    def coefficients(i):
        row = rows - COARSE_DEGREE + i
        g = g_ref[row]
        whole = coarsen_packed(positive(g), pair_ref.at[3 * i]) > 0.75
        first = (lane_index(whole.shape) & 3) == 0
        cg[i] = jnp.where(whole & first, coarsen_packed(g, pair_ref.at[3 * i + 1]), 0.0)
        ca[i] = coarsen_packed(a_ref[row], pair_ref.at[3 * i + 2])

    rows_loop(0, coarse_rows, coefficients, block=10)
    level_setup(1, coarse_rows - 1, 4, STEP_SCALE / 16.0, cg, ca, cwx, cwy, cwz, cinv, cd, wb_ref=cwb)


def coarse_kernel(slots, *refs):
    own_refs, around_refs, refs = refs[: 1 + slots], refs[1 + slots : 2 + 2 * slots], refs[2 + 2 * slots :]
    wx, wy, wz, wb, inv, d_ref, cwx, cwy, cwz, cwb, cinv, mid_out, coarse_out = refs[:13]
    b_ref, e_ref, u0, u1, u2, u3, cb, ce, v0, v1, v2, v3, v4, v5, pair_ref = refs[13:]
    rows, ny, nz = own_refs[0].shape
    unread = rows - around_refs[0].shape[1]
    for start, slot, s_ref in placed_parts(slots, rows, own_refs, around_refs, unread):
        at = slice(slot * ny, (slot + 1) * ny)
        for j in range(s_ref.shape[0]):
            b_ref[start + j, at] = s_ref[j]

    reach = 2 * (COARSE_DEGREE - 1)
    u_refs = (u0, u1, u2, u3)
    updates = [Circular(u_ref) for u_ref in u_refs]
    level_sweeps(rows, rows, reach, DEGREE, SMOOTH_LOW, True, 2, b_ref, inv, wx, wy, wz, e_ref, updates, True, wb)

    total = u0[rows : 2 * rows, TILE : TILE + ny]
    for u_ref in u_refs[1:]:
        total = total + u_ref[rows : 2 * rows, TILE : TILE + ny]
    total = total.reshape(rows * ny, nz)
    for t in range(2):
        lines = compact(total, 2, t).reshape(rows, ny, nz // 2)
        for j in range(rows):
            mid_out[2 * j + t] = lines[j]

    half, cny = rows, ny // 2
    cbase = COARSE_DEGREE
    def source(i):
        row = rows - cbase + i
        cb[i] = coarsen_packed(d_ref[row] * e_ref[row], pair_ref.at[i])

    rows_loop(1, half + 2 * cbase - 1, source)
    v_refs = (v0, v1, v2, v3, v4, v5)
    updates = [Circular(v_ref) for v_ref in v_refs]
    weights = (cinv, cwx, cwy, cwz)
    level_sweeps(cbase, half, 0, COARSE_DEGREE, COARSE_LOW, False, 4, cb, *weights, ce, updates, wb_ref=cwb)
    total = v0[cbase : cbase + half, TILE : TILE + cny]
    for v_ref in v_refs[1:]:
        total = total + v_ref[cbase : cbase + half, TILE : TILE + cny]
    coarse_out[...] = compact(total.reshape(half * cny, nz), 4).reshape(half, cny, nz // 4)


def call(kernel, ins, outs, scratch=(), in_hbm=0, out_hbm=0):
    vmem, hbm = pl.BlockSpec(memory_space=pltpu.VMEM), pl.BlockSpec(memory_space=pltpu.HBM)
    return pl.pallas_call(
        kernel,
        out_shape=[jax.ShapeDtypeStruct(shape, jnp.float32) for shape in outs],
        in_specs=[hbm] * in_hbm + [vmem] * (len(ins) - in_hbm),
        out_specs=[hbm] * out_hbm + [vmem] * (len(outs) - out_hbm),
        scratch_shapes=[pltpu.VMEM(shape, jnp.float32) if isinstance(shape, tuple) else shape for shape in scratch],
        compiler_params=pltpu.CompilerParams(vmem_limit_bytes=VMEM_BYTES),
    )(*ins)


def body(source, conductivity, absorption, brick_mask):
    doms, grps = lax.axis_size("dom"), lax.axis_size("grp")
    slots = min(grps - 1, 2)
    nx, ny, nz = source.shape
    lower, upper = DEGREE, DEGREE + 1

    def pairing(first):
        pairs = [(i, i + 1) for i in range(first, doms - 1, 2)]
        return pairs + [(j, i) for i, j in pairs]

    def swap_even(array):
        return lax.ppermute(array, "dom", pairing(0))

    def swap_odd(array):
        return lax.ppermute(array, "dom", pairing(1))

    downward = [(i + 1, i) for i in range(grps - 1)]
    upward = [(i, i + 1) for i in range(grps - 1)]

    def along_grp(arrays):
        if slots == 0:
            return []
        if slots == 1:
            return [lax.ppermute(arrays[0], "grp", downward + upward)]
        return [lax.ppermute(arrays[0], "grp", downward), lax.ppermute(arrays[-1], "grp", upward)]

    crossing = []
    for i in range(doms - 1):
        crossing += [(i * grps, (i + 1) * grps + 1), ((i + 1) * grps + 1, i * grps)]

    def send_around(own, beside, spare=0):
        if slots == 1:
            both = stack([own, beside[0]], spare=spare)
            return [lax.ppermute(both, ("dom", "grp"), crossing)], both
        return [swap_even(own), swap_odd(own)], own

    def share_around(arrays, *earlier):
        both = stack(arrays, *earlier)
        both = both.reshape(2, *both.shape[-3:])
        return [both, *along_grp([both])]

    fields = [pltpu.with_memory_space_constraint(x, pltpu.HBM) for x in (source, conductivity, absorption, brick_mask)]
    bricks = pltpu.VMEM(brick_mask.shape, brick_mask.dtype)
    payload = (2 * lower + upper, ny, nz)
    packed = nx // 4
    small = (packed, ny // 2, nz)
    b_own, a_own, g_own, to_even, to_odd, coeffs, *edges = call(
        functools.partial(block_kernel, slots),
        fields,
        [source.shape] * 3 + [payload] * 2 + [(2 * packed, ny // 2, nz)] + [(3, nx, TILE, nz)] * slots,
        [bricks, (4 * packed, ny, nz), pltpu.SemaphoreType.DMA((4,))],
        in_hbm=4,
    )
    from_even, from_odd = swap_even(to_even), swap_odd(to_odd)
    own = (b_own, a_own, g_own, *along_grp(edges))
    coeffs_beside = along_grp([coeffs])
    coeffs_sent, _ = send_around(coeffs, coeffs_beside)

    wide = (nx, ny + slots * TILE, nz)
    pairs = (nx // 2, ny, nz)
    *state, it_inner, res_inner, s_inner = call(
        functools.partial(inner_kernel, slots),
        own,
        [wide] * 10 + [source.shape, source.shape, small],
        [pairs],
    )
    corners = call(
        functools.partial(corner_kernel, slots),
        (from_even, from_odd, s_inner),
        [(2, payload[0], TILE, nz)] * slots,
    )
    corners_beside = along_grp(corners)
    rim = (2 * upper, ny, nz)
    near = (4 * upper + 2, ny + slots * TILE, nz)
    it_rim, res_rim, mid_source = call(
        functools.partial(rim_kernel, slots),
        (*own, *state, res_inner, s_inner, from_even, from_odd, *corners_beside),
        [rim, rim, small],
        [near] * 13 + [pairs],
    )
    fine_iterate, fine_residual, written = call(
        output_kernel,
        (it_inner, res_inner, it_rim, res_rim),
        [source.shape, source.shape, (TILE, nz)],
        [pltpu.SemaphoreType.DMA((6,))],
        out_hbm=2,
    )

    source_beside = along_grp([mid_source])
    unread = packed - -(-(2 * (COARSE_DEGREE - 1) + DEGREE) // 2)
    source_sent, sending = send_around(mid_source, source_beside, unread)
    q_ins = [coeffs, *coeffs_beside, *share_around(coeffs_sent, sending)]
    mid_y = (1 + slots) * ny // 2
    mid_wide = (3 * packed, mid_y, nz)
    coarse_rows = nx // 4 + 2 * COARSE_DEGREE
    coarse_wide = (coarse_rows, mid_y // 2, nz)
    weights = call(
        functools.partial(coefficient_kernel, slots),
        q_ins,
        [mid_wide] * 6 + [coarse_wide] * 5,
        [mid_wide] * 2 + [coarse_wide] * 3 + [(3 * coarse_rows, mid_y, nz)],
    )
    s_ins = [mid_source, *source_beside, *share_around(source_sent, weights[-1], written)]
    mid_iterate, coarse_iterate = call(
        functools.partial(coarse_kernel, slots),
        (*s_ins, *weights),
        [(nx // 2, ny // 2, nz // 2), (nx // 4, ny // 4, nz // 4)],
        [mid_wide] * 2 + [(3 * packed, mid_y + 2 * TILE, nz)] * 4 + [coarse_wide] * 2 + [(coarse_rows, mid_y // 2 + 2 * TILE, nz)] * 6 + [(coarse_rows, mid_y, nz)],
    )
    return (fine_iterate, fine_residual, mid_iterate, coarse_iterate)


def solution(mesh):
    spec = P("dom", "grp", None)
    return jax.shard_map(body, mesh=mesh, in_specs=(spec,) * 4, out_specs=(spec,) * 4, check_vma=False)
```
